32 devices in a mesh: dp: 4 (over y, x), expert: 8 (over z, core).
Axes of the slice: x: 2, y: 2, z: 4, core: 2. Of those that a mesh axis runs over, the one named last changes fastest.
Arguments:
- activations: bfloat16 [4096, 4096], P(('dp', 'expert')), may hold values from -6 to 6
- cotangent: bfloat16 [4096, 4096], P(('dp', 'expert')), may hold values from -6 to 6
- basis: bfloat16 [4096, 512], replicated, may hold values from -0.09375 to 0.09375
- route_ids: int32 [4096, 8], P(('dp', 'expert')), may hold values from 0 to 15, all different within a row; in each aligned block of 128 rows (0 to 127, 128 to 255, ...) at most 96 rows name the same one
- route_weights: float32 [4096, 8], P(('dp', 'expert')), may hold values from 0.05 to 0.5
- proj_in: bfloat16 [16, 512, 128], P('expert'), may hold values from -0.25 to 0.25
- gate_factor: bfloat16 [16, 128, 1536], P('expert'), may hold values from -0.5 to 0.5
- up_factor: bfloat16 [16, 128, 1536], P('expert'), may hold values from -0.5 to 0.5
- down_factor: bfloat16 [16, 1536, 128], P('expert'), may hold values from -0.15625 to 0.15625
- proj_out: bfloat16 [16, 128, 512], P('expert'), may hold values from -0.5 to 0.5
Outputs:
- grad_input: bfloat16 [4096, 4096], P(('dp', 'expert'))
- grad_route: float32 [4096, 8], P(('dp', 'expert'))
- grad_basis: float32 [4096, 512], P(('dp', 'expert'))
- grad_proj_in: float32 [16, 512, 128], P('expert', 'dp')
- grad_gate: float32 [16, 128, 1536], P('expert', None, 'dp')
- grad_up: float32 [16, 128, 1536], P('expert', None, 'dp')
- grad_down: float32 [16, 1536, 128], P('expert', 'dp')
- grad_proj_out: float32 [16, 128, 512], P('expert', None, 'dp')
The draws below stay inside these ranges and needn't reach their ends.
Inputs may be any that keep to these rules, and one draw needn't show every extreme that they name: `route_ids`: among the 128 rows of one device no expert is named by more than 96 of them, a bound that some block reaches; each row names 8 different experts.
All inputs are finite; a program needn't handle non-finite values.
Results may differ from the reference program's by a relative error of at most 0.025.
Values may be sent and summed in bfloat16 or wider, within the bound.
A program may use at most 128 MiB of HBM per device.

```python
import math
import jax
import jax.numpy as jnp
import numpy as np
from jax import lax

D = 4096
FF = 1536
R = 512
K = 128
TOP = 8
TOK_DEV = 128
EXPERTS = 16
TOKENS = 4096
CAP = 96


def strengthened(array, own_key, source, target, blocks, factor):
    def block_of(axis_at):
        return (jnp.arange(array.shape[axis_at]) // (array.shape[axis_at] // blocks)).reshape((-1,) + (1,) * (array.ndim - 1 - axis_at))

    one_side = jax.random.permutation(own_key, blocks)[block_of(target)]
    other_side = (block_of(target) + blocks // 2) % blocks
    return jnp.where((block_of(source) == one_side) | (block_of(source) == other_side), factor * array, array)


def levels(rng, shape, pieces, least, largest):
    def one(axis_at, shards_of):
        heights = jax.random.uniform(jax.random.fold_in(jax.random.fold_in(rng, 6), axis_at), (shards_of,), jnp.float32, least / len(pieces), largest / len(pieces))
        return jnp.repeat(jnp.exp(heights), shape[axis_at] // shards_of).reshape((-1,) + (1,) * (len(shape) - axis_at - 1))

    level = one(*pieces[0])
    for cut in pieces[1:]:
        level = level * one(*cut)
    return level


def routed_block(stream_key, own, number, rows, number_of, top, most, skew):
    order = jax.random.permutation(stream_key, number_of)
    packed, ordinary = portions_of(number_of, rows * top, most, skew, True), portions_of(number_of, rows * top, most, skew, False)
    places = jnp.arange(number_of)

    def named(lengths, offset_by):
        used = int((lengths > 0).sum())
        fixed = max(1, used // 4)
        moved = fixed + (places - fixed + offset_by * (used - fixed)) % max(1, number_of - fixed)
        return jnp.zeros((number_of,), jnp.int32).at[order[jnp.where(places < fixed, places, moved)]].set(jnp.asarray(lengths, jnp.int32))

    lengths = jnp.where(number % 4 == 0, named(packed, number // 4), named(ordinary, number - number // 4 - 1))
    mixed = jax.random.permutation(jax.random.fold_in(own, 3), number_of)
    donor, receiver = mixed[0:number_of // 2 * 2:2], mixed[1:number_of // 2 * 2:2]
    margin = jnp.minimum(lengths[donor] - 1, most - lengths[receiver]) // 2
    margin = jnp.where((donor == order[0]) | (receiver == order[0]) | (lengths[receiver] == 0), 0, jnp.maximum(margin, 0))
    moved = jax.random.randint(jax.random.fold_in(own, 4), (number_of // 2,), 0, 1 << 20) % (margin + 1)
    lengths = lengths.at[donor].add(-moved).at[receiver].add(moved)
    labels = jnp.searchsorted(jnp.cumsum(lengths), jnp.arange(rows * top), side="right").astype(jnp.int32)
    listing = labels.reshape(top, rows).T
    listing = listing[jax.random.permutation(jax.random.fold_in(own, 1), rows)]
    offset_by = jax.random.randint(jax.random.fold_in(own, 2), (rows, 1), 0, top)
    return jnp.take_along_axis(listing, (jnp.arange(top)[None, :] + offset_by) % top, axis=1)


def portions_of(count, total, reach, skew, full):
    portions = [(1 << 20) // math.isqrt(grade ** skew) + 1 for grade in range(1, count + 1)]
    largest = reach if full else min(reach, max(-(-total // count), total * portions[0] // sum(portions)))
    least = 1 if total - largest >= count - 1 else 0
    given, surplus = [largest] + [least] * (count - 1), total - largest - least * (count - 1)
    while surplus > 0:
        movable = [i for i in range(1, count) if given[i] < largest] or [i for i in range(1, count) if given[i] < reach]
        pool, remaining = sum([portions[i] for i in movable]), surplus
        for i in movable:
            more = min(reach - given[i], max(1, remaining * portions[i] // pool), surplus)
            given[i] = given[i] + more
            surplus = surplus - more
    return np.array(given)


def scatter_about(stream_key, dims, spread, limit, shards=(), kind=jnp.bfloat16):
    gain = levels(stream_key, dims, shards, -0.22, 0.18) if shards else 1.0
    result = jax.random.normal(stream_key, dims, jnp.float32) * spread * gain
    return jnp.minimum(jnp.maximum(result, -limit), limit).astype(kind)


def bell_draw_with(rng, dims, deviation, reach, pieces, heavy, held_as=jnp.bfloat16):
    drawn = deviation * jax.random.normal(rng, dims, jnp.float32)
    if pieces:
        drawn = drawn * levels(rng, dims, pieces, -0.22, 0.18)
    return jnp.clip(strengthened(drawn, jax.random.fold_in(rng, 3), *heavy), -reach, reach).astype(held_as)


def setup_inputs(seed: int = 0) -> dict:
    seeds = jax.random.split(jax.random.key(seed), 11)
    activations = bell_draw_with(seeds[0], (TOKENS, D), 1.0, 6.0, ((0, 32),), (0, 1, 32, 2.75))
    cotangent = bell_draw_with(seeds[1], (TOKENS, D), 1.0, 6.0, ((0, 32),), (0, 1, 32, 2.75))
    basis = scatter_about(seeds[2], (D, R), D ** -0.5, 0.09375)
    route_ids_keys = jax.random.split(jax.random.fold_in(seeds[3], 1), TOKENS // TOK_DEV)
    route_ids_turns = jax.random.permutation(jax.random.fold_in(seeds[3], 3), TOKENS // TOK_DEV)
    route_ids = jax.vmap(lambda own, number: routed_block(jax.random.fold_in(seeds[3], 2), own, number, TOK_DEV, EXPERTS, TOP, CAP, 2))(route_ids_keys, route_ids_turns).reshape((TOKENS, TOP))
    route_weights = jnp.clip(jnp.exp(math.log(0.5) - 2.3025851 * jax.random.uniform(seeds[4], (TOKENS, TOP), jnp.float32) ** levels(seeds[4], (TOKENS, TOP), ((0, 32),), -0.2, 0.2)), 0.05, 0.5)
    proj_in = scatter_about(seeds[5], (EXPERTS, R, K), R ** -0.5, 0.25, ((0, 8),))
    gate_factor = scatter_about(seeds[6], (EXPERTS, K, FF), K ** -0.5, 0.5, ((0, 8),))
    up_factor = scatter_about(seeds[7], (EXPERTS, K, FF), K ** -0.5, 0.5, ((0, 8),))
    down_factor = scatter_about(seeds[8], (EXPERTS, FF, K), FF ** -0.5, 0.15625, ((0, 8),))
    proj_out = scatter_about(seeds[9], (EXPERTS, K, R), K ** -0.5, 0.5, ((0, 8),))
    return dict(activations=activations, cotangent=cotangent, basis=basis, route_ids=route_ids, route_weights=route_weights, proj_in=proj_in, gate_factor=gate_factor, up_factor=up_factor, down_factor=down_factor, proj_out=proj_out)


def silu_parts(pre):
    sig = jax.nn.sigmoid(pre)
    return pre * sig, sig * (1.0 + pre * (1.0 - sig))


def expert_rows(coords, scaled, proj_in, gate_factor, up_factor, down_factor, proj_out):
    f32 = jnp.float32
    codes = jnp.dot(coords, proj_in, preferred_element_type=f32).astype(jnp.bfloat16)
    gate_pre = jnp.dot(codes, gate_factor, preferred_element_type=f32)
    up_pre = jnp.dot(codes, up_factor, preferred_element_type=f32)
    active, slope = silu_parts(gate_pre)
    hidden = (active * up_pre).astype(jnp.bfloat16)
    narrow = jnp.dot(hidden, down_factor, preferred_element_type=f32).astype(jnp.bfloat16)
    outcome = jnp.dot(narrow, proj_out, preferred_element_type=f32).astype(jnp.bfloat16)
    g_out = jnp.dot(narrow.T, scaled, preferred_element_type=f32)
    d_narrow = jnp.dot(scaled, proj_out.T, preferred_element_type=f32).astype(jnp.bfloat16)
    g_down = jnp.dot(hidden.T, d_narrow, preferred_element_type=f32)
    d_hidden = jnp.dot(d_narrow, down_factor.T, preferred_element_type=f32)
    d_gate = (d_hidden * up_pre * slope).astype(jnp.bfloat16)
    d_up = (d_hidden * active).astype(jnp.bfloat16)
    g_gate = jnp.dot(codes.T, d_gate, preferred_element_type=f32)
    g_up = jnp.dot(codes.T, d_up, preferred_element_type=f32)
    d_codes = (jnp.dot(d_gate, gate_factor.T, preferred_element_type=f32)
               + jnp.dot(d_up, up_factor.T, preferred_element_type=f32)).astype(jnp.bfloat16)
    g_in = jnp.dot(coords.T, d_codes, preferred_element_type=f32)
    d_coords = jnp.dot(d_codes, proj_in.T, preferred_element_type=f32).astype(jnp.bfloat16)
    return outcome, d_coords, (g_in, g_gate, g_up, g_down, g_out)


def reference(activations, cotangent, basis, route_ids, route_weights, proj_in, gate_factor, up_factor, down_factor, proj_out):
    f32 = jnp.float32
    coords = jnp.dot(activations, basis, preferred_element_type=f32).astype(jnp.bfloat16)
    back = jnp.dot(cotangent, basis, preferred_element_type=f32).astype(jnp.bfloat16)
    sources = TOKENS // TOK_DEV
    blocks = route_ids.reshape(sources, TOK_DEV * TOP).astype(jnp.int32)

    def slots_of(block):
        onehot = (block[:, None] == jnp.arange(EXPERTS, dtype=jnp.int32)[None, :]).astype(jnp.int32)
        return (jnp.sum(jnp.cumsum(onehot, axis=0) * onehot, axis=1) - 1).astype(jnp.int32)

    slots = lax.map(slots_of, blocks)
    anchor = jnp.arange(sources, dtype=jnp.int32)[:, None]
    place = (blocks * (sources * CAP) + anchor * CAP + slots).reshape(-1).astype(jnp.int32)
    total = TOKENS * TOP
    table = jnp.full((EXPERTS * sources * CAP,), total, jnp.int32)
    table = table.at[place].set(jnp.arange(total, dtype=jnp.int32)).reshape(EXPERTS, sources * CAP)
    coords_pad = jnp.concatenate([coords, jnp.zeros((1, R), jnp.bfloat16)], axis=0)
    back_pad = jnp.concatenate([back, jnp.zeros((1, R), jnp.bfloat16)], axis=0)
    weight_pad = jnp.concatenate([route_weights.reshape(-1).astype(f32), jnp.zeros((1,), f32)], axis=0)

    def step(carry, inputs):
        grad_coords, mixed, grad_route = carry
        entry, p_in, g_fac, u_fac, d_fac, p_out = inputs
        token = (entry // TOP).astype(jnp.int32)
        rows = coords_pad[token]
        weight = weight_pad[entry]
        back_rows = back_pad[token].astype(f32)
        scaled = (weight[:, None] * back_rows).astype(jnp.bfloat16)
        outcome, d_coords, grads = expert_rows(rows, scaled, p_in, g_fac, u_fac, d_fac, p_out)
        outcome32 = outcome.astype(f32)
        grad_coords = grad_coords.at[token].add(d_coords.astype(f32), mode="drop")
        mixed = mixed.at[token].add(weight[:, None] * outcome32, mode="drop")
        grad_route = grad_route.at[entry].add(jnp.sum(back_rows * outcome32, axis=1), mode="drop")
        return (grad_coords, mixed, grad_route), grads

    start = (jnp.zeros((TOKENS, R), f32), jnp.zeros((TOKENS, R), f32), jnp.zeros((total,), f32))
    (grad_coords, mixed, grad_route), grads = lax.scan(
        step, start, (table, proj_in, gate_factor, up_factor, down_factor, proj_out))
    dz = grad_coords.astype(jnp.bfloat16)
    mixed_b = mixed.astype(jnp.bfloat16)
    grad_input = jnp.dot(dz, basis.T, preferred_element_type=f32).astype(jnp.bfloat16)
    grad_basis = (jnp.dot(activations.T, dz, preferred_element_type=f32)
                  + jnp.dot(cotangent.T, mixed_b, preferred_element_type=f32))
    return (grad_input, grad_route.reshape(TOKENS, TOP), grad_basis,
            grads[0], grads[1], grads[2], grads[3], grads[4])
```

```python
import functools

import jax
import jax.numpy as jnp
from jax import lax
from jax.experimental import pallas as pl
from jax.experimental.pallas import tpu as pltpu
from jax.sharding import PartitionSpec as P

EXP_DEV = 2
TOK_DEV = 128
LANES = 128
VMEM_LIMIT = 58 * 1024 * 1024
MESH = pl.DeviceIdType.MESH
f32 = jnp.float32
bf16 = jnp.bfloat16


def remote(src, dst, send, recv, **device):
    return pltpu.make_async_remote_copy(
        src_ref=src, dst_ref=dst, send_sem=send, recv_sem=recv, device_id=device, device_id_type=MESH
    )


def dot(a, b):
    return jnp.dot(a, b, preferred_element_type=f32)


def dot_nt(a, b):
    return lax.dot_general(a, b, (((1,), (1,)), ((), ())), preferred_element_type=f32)


def dot_tn(a, b):
    return lax.dot_general(a, b, (((0,), (0,)), ((), ())), preferred_element_type=f32)


def loop(low, high, body):
    def step(i, carry):
        body(i)
        return carry

    lax.fori_loop(low, high, step, 0)


def greet(n, n_dp, me, p):
    barrier = pltpu.get_barrier_semaphore()

    def expert_peer(d):
        pl.semaphore_signal(
            barrier, inc=1, device_id={"expert": lax.rem(me + d, n)}, device_id_type=MESH
        )

    def dp_peer(d):
        pl.semaphore_signal(
            barrier, inc=1, device_id={"dp": lax.rem(p + d, n_dp)}, device_id_type=MESH
        )

    loop(1, n, expert_peer)
    loop(1, n_dp, dp_peer)
    pl.semaphore_wait(barrier, n - 1 + n_dp - 1)


def gather_kernel(
    n, n_dp, act, cot, basis, wt, x_out, w_out, cols_out, s_c, r_c, s_x, r_x, s_f, s_w, r_w
):
    me, p = lax.axis_index("expert"), lax.axis_index("dp")
    nz = n // 2
    core, z = lax.rem(me, 2), me // 2
    sib = me + 1 - 2 * core
    width = act.shape[1] // n_dp
    greet(n, n_dp, me, p)

    def w_copy(d):
        return remote(
            wt.at[lax.rem(me + d, n)], w_out.at[me], s_w.at[d], r_w.at[me], expert=lax.rem(me + d, n)
        )

    loop(1, n, lambda d: w_copy(d).start())

    def x_copy(a, d, to):
        return remote(x_out.at[me, a], x_out.at[me, a], s_x.at[a, d], r_x.at[a, me], expert=to)

    def line_peer(d):
        return lax.rem(z + d, nz) * 2 + core

    for a, ref in enumerate((act, cot)):
        x_out[me, a] = dot(ref[...], basis[...]).astype(bf16)
        loop(1, nz, lambda d: x_copy(a, d, line_peer(d)).start())
        x_copy(a, 0, sib).start()

    def col_copy(a, d):
        q = lax.rem(p + d, n_dp)
        ref = (act, cot)[a]
        return remote(
            ref.at[:, pl.ds(pl.multiple_of(q * width, LANES), width)],
            cols_out.at[p, a],
            s_c.at[a, d],
            r_c.at[a, p],
            dp=q,
        )

    for a in range(2):
        loop(1, n_dp, lambda d: col_copy(a, d).start())
    for a, ref in enumerate((act, cot)):
        cols_out[p, a] = ref[:, pl.ds(pl.multiple_of(p * width, LANES), width)]
    w_out[me] = wt[me]

    def forward(a, d):
        src = lax.rem(z + nz - d, nz) * 2 + core
        return remote(x_out.at[src, a], x_out.at[src, a], s_f.at[a, d], r_x.at[a, src], expert=sib)

    def pass_on(a, d):
        forward(a, d).wait_recv()
        forward(a, d).start()

    for a in range(2):
        loop(1, nz, lambda d: pass_on(a, d))

    def sib_wait(a, k):
        src = k * 2 + 1 - core
        remote(
            x_out.at[src, a], x_out.at[src, a], s_f.at[a, 0], r_x.at[a, src], expert=sib
        ).wait_recv()

    def w_wait(d):
        src = lax.rem(me + n - d, n)
        remote(wt.at[src], w_out.at[src], s_w.at[d], r_w.at[src], expert=src).wait_recv()

    def col_wait(a, d):
        src = lax.rem(p + n_dp - d, n_dp)
        remote(cols_out.at[src, a], cols_out.at[src, a], s_c.at[a, d], r_c.at[a, src], dp=src).wait_recv()

    loop(1, n, w_wait)
    for a in range(2):
        loop(0, nz, lambda k: sib_wait(a, k))
        loop(1, n_dp, lambda d: col_wait(a, d))
    loop(1, n, lambda d: w_copy(d).wait_send())
    for a in range(2):
        x_copy(a, 0, sib).wait_send()
        loop(1, nz, lambda d: x_copy(a, d, line_peer(d)).wait_send())
        loop(1, nz, lambda d: forward(a, d).wait_send())
        loop(1, n_dp, lambda d: col_copy(a, d).wait_send())


def expert_kernel(n_dp, chunk, x, w, pin, gate, up, down, pout, part, route, packed, acc):
    step = pl.program_id(0)
    nb, rank = x.shape[0], x.shape[3]
    rows = nb * TOK_DEV
    ff = gate.shape[2]

    @pl.when(step == 0)
    def _():
        acc[...] = jnp.zeros_like(acc)

    coords = x[:, 0].reshape(rows, rank)
    back = x[:, 1].reshape(rows, rank).astype(f32)
    dz = jnp.zeros((rows, rank), f32)
    mixed = jnp.zeros((rows, rank), f32)
    dots = jnp.zeros((8, rows), f32)
    line = lax.broadcasted_iota(jnp.int32, (8, rows), 0)
    for e in range(EXP_DEV):
        we = w[:, e : e + 1]
        scaled = (we * back).astype(bf16)
        codes = dot(coords, pin[e]).astype(bf16)
        d_narrow32 = dot_nt(scaled, pout[e])
        d_narrow = d_narrow32.astype(bf16)
        codes_t, d_narrow_t = codes.T, d_narrow.T
        narrow32 = jnp.zeros((rows, LANES), f32)
        d_codes32 = jnp.zeros((rows, LANES), f32)
        for at in range(0, ff, chunk):
            now = slice(at, at + chunk)
            gate_pre = dot(codes, gate[e, :, now])
            up_pre = dot(codes, up[e, :, now])
            d_hidden = dot_nt(d_narrow, down[e, now, :])
            sig = 0.5 * jnp.tanh(0.5 * gate_pre) + 0.5
            active = gate_pre * sig
            slope = sig + active * (1.0 - sig)
            hidden = (active * up_pre).astype(bf16)
            d_gate = (d_hidden * up_pre * slope).astype(bf16)
            d_up = (d_hidden * active).astype(bf16)
            narrow32 += dot(hidden, down[e, now, :])
            d_codes32 += dot_nt(d_gate, gate[e, :, now]) + dot_nt(d_up, up[e, :, now])
            acc[e, :, at : at + chunk] += dot(codes_t, d_gate)
            acc[e, :, ff + at : ff + at + chunk] += dot(codes_t, d_up)
            acc[e, :, 2 * ff + at : 2 * ff + at + chunk] += dot(d_narrow_t, hidden)
        narrow = narrow32.astype(bf16)
        d_codes = d_codes32.astype(bf16)
        outcome = dot(narrow, pout[e]).astype(bf16)
        mixed += we * outcome.astype(f32)
        dz += dot_nt(d_codes, pin[e])
        acc[e, :, 3 * ff : 3 * ff + rank] += dot(d_codes.T, coords)
        acc[e, :, 3 * ff + rank :] += dot(narrow.T, scaled)
        product = narrow.astype(f32) * d_narrow32
        sums = lax.dot_general(
            jnp.ones((8, LANES), f32),
            product,
            (((1,), (1,)), ((), ())),
            precision=lax.Precision.HIGHEST,
            preferred_element_type=f32,
        )
        dots = jnp.where(line == e, sums, dots)
    part[:, 0] = dz.astype(bf16).reshape(nb, TOK_DEV, rank)
    part[:, 1] = mixed.astype(bf16).reshape(nb, TOK_DEV, rank)
    for b in range(nb):
        route[b] = dots[:, b * TOK_DEV : (b + 1) * TOK_DEV]

    @pl.when(step == pl.num_programs(0) - 1)
    def _():
        wide, deep = ff // n_dp, rank // n_dp
        for q in range(n_dp):
            for e in range(EXP_DEV):
                starts = [3 * ff + q * deep + i for i in range(0, deep, LANES)]
                for base in (0, ff, 2 * ff):
                    starts += [base + q * wide + i for i in range(0, wide, LANES)]
                starts += [3 * ff + rank + q * deep + i for i in range(0, deep, LANES)]
                for i, at in enumerate(starts):
                    packed[q, e, i] = acc[e, :, at : at + LANES].astype(bf16)


def expert_sum(n, me, part, held, landed, total, s1, r1, s2, r2):
    nz = n // 2
    core, z = lax.rem(me, 2), me // 2
    sib = me + 1 - 2 * core

    def to_sib(k):
        return remote(part.at[k * 2 + 1 - core], held.at[k], s1.at[k], r1.at[k], expert=sib)

    def to_line(d):
        k = lax.rem(z + d, nz)
        return remote(held.at[k], landed.at[z], s2.at[d], r2.at[z], expert=k * 2 + core)

    loop(1, nz, lambda d: to_sib(lax.rem(z + d, nz)).start())
    to_sib(z).start()

    def add(d):
        k = lax.rem(z + d, nz)
        to_sib(k).wait_recv()
        held[k] = (part[k * 2 + core].astype(f32) + held[k].astype(f32)).astype(bf16)
        to_line(d).start()

    loop(1, nz, add)
    to_sib(z).wait_recv()
    total[...] = part[me].astype(f32) + held[z].astype(f32)

    def collect(d):
        k = lax.rem(z + nz - d, nz)
        remote(held.at[k], landed.at[k], s2.at[d], r2.at[k], expert=k * 2 + core).wait_recv()
        total[...] += landed[k].astype(f32)

    loop(1, nz, collect)
    loop(0, nz, lambda k: to_sib(k).wait_send())
    loop(1, nz, lambda d: to_line(d).wait_send())


def combine_kernel(
    n,
    n_dp,
    part,
    route,
    packed,
    cols,
    basis,
    grad_input,
    grad_basis,
    grads,
    route_out,
    held,
    landed,
    total,
    dzm,
    block,
    held_b,
    landed_b,
    grads_in,
    s_g,
    r_g,
    s_r,
    r_r,
    s1,
    r1,
    s2,
    r2,
    s_d,
    r_d,
    t1,
    q1,
    t2,
    q2,
):
    me, p = lax.axis_index("expert"), lax.axis_index("dp")
    rank = basis.shape[1]
    greet(n, n_dp, me, p)

    def route_copy(d):
        j = lax.rem(me + d, n)
        return remote(route.at[j], route_out.at[me], s_r.at[d], r_r.at[me], expert=j)

    def grad_copy(d):
        q = lax.rem(p + d, n_dp)
        return remote(packed.at[q], grads_in.at[p], s_g.at[d], r_g.at[p], dp=q)

    loop(1, n, lambda d: route_copy(d).start())
    loop(1, n_dp, lambda d: grad_copy(d).start())
    route_out[me] = route[me]
    expert_sum(n, me, part, held, landed, total, s1, r1, s2, r2)
    dzm[p] = total[...].astype(bf16)

    def dzm_copy(d):
        q = lax.rem(p + d, n_dp)
        return remote(dzm.at[p], dzm.at[p], s_d.at[d], r_d.at[p], dp=q)

    loop(1, n_dp, lambda d: dzm_copy(d).start())
    grad_input[...] = dot_nt(dzm[p, 0], basis[...]).astype(bf16)

    def dzm_wait(d):
        src = lax.rem(p + n_dp - d, n_dp)
        remote(dzm.at[src], dzm.at[src], s_d.at[d], r_d.at[src], dp=src).wait_recv()

    loop(1, n_dp, dzm_wait)
    tokens = n_dp * 2 * TOK_DEV
    width = cols.shape[3]
    sums = dot_tn(cols[...].reshape(tokens, width), dzm[...].reshape(tokens, rank))
    block[...] = sums.astype(bf16).reshape(block.shape)
    expert_sum(n, me, block, held_b, landed_b, grad_basis, t1, q1, t2, q2)

    def grad_wait(d):
        src = lax.rem(p + n_dp - d, n_dp)
        remote(grads_in.at[src], grads_in.at[src], s_g.at[d], r_g.at[src], dp=src).wait_recv()
        grads[...] += grads_in[src].astype(f32)

    grads[...] = packed[p].astype(f32)
    loop(1, n_dp, grad_wait)

    def route_wait(d):
        src = lax.rem(me + n - d, n)
        remote(route.at[src], route_out.at[src], s_r.at[d], r_r.at[src], expert=src).wait_recv()

    loop(1, n, route_wait)
    loop(1, n, lambda d: route_copy(d).wait_send())
    loop(1, n_dp, lambda d: grad_copy(d).wait_send())
    loop(1, n_dp, lambda d: dzm_copy(d).wait_send())


def per_device(
    n,
    n_dp,
    activations,
    cotangent,
    basis,
    route_ids,
    route_weights,
    proj_in,
    gate_factor,
    up_factor,
    down_factor,
    proj_out,
):
    model, rank = basis.shape
    ff = gate_factor.shape[2]
    nz = n // 2
    experts = EXP_DEV * n
    width = model // n_dp
    vmem = pl.BlockSpec(memory_space=pltpu.VMEM)
    dma = pltpu.SemaphoreType.DMA

    chosen = route_ids[:, None, :] == jnp.arange(experts, dtype=jnp.int32)[None, :, None]
    dense = jnp.sum(jnp.where(chosen, route_weights[:, None, :], 0.0), axis=2)
    wt = dense.T.reshape(n, EXP_DEV, TOK_DEV)
    wt = jnp.pad(wt, ((0, 0), (0, 8 - EXP_DEV), (0, 0)))

    x, w_all, cols = pl.pallas_call(
        functools.partial(gather_kernel, n, n_dp),
        out_shape=(
            jax.ShapeDtypeStruct((n, 2, TOK_DEV, rank), bf16),
            jax.ShapeDtypeStruct((n, 8, TOK_DEV), f32),
            jax.ShapeDtypeStruct((n_dp, 2, TOK_DEV, width), bf16),
        ),
        in_specs=[vmem] * 4,
        out_specs=(vmem,) * 3,
        scratch_shapes=[
            dma((2, n_dp)),
            dma((2, n_dp)),
            dma((2, nz)),
            dma((2, n)),
            dma((2, nz)),
            dma((n,)),
            dma((n,)),
        ],
        compiler_params=pltpu.CompilerParams(
            collective_id=0, has_side_effects=True, vmem_limit_bytes=VMEM_LIMIT
        ),
        name="gather_tokens",
    )(activations, cotangent, basis, wt)

    w_rows = w_all.transpose(0, 2, 1).reshape(n * TOK_DEV, 8)
    nb = 2
    blocks = EXP_DEV, (2 * rank + 3 * ff) // n_dp // LANES, LANES, LANES
    whole = lambda a: pl.BlockSpec(a.shape, lambda i: (0,) * a.ndim)
    part, route, packed = pl.pallas_call(
        functools.partial(expert_kernel, n_dp, ff // 3),
        grid=(n // nb,),
        out_shape=(
            jax.ShapeDtypeStruct((n, 2, TOK_DEV, rank), bf16),
            jax.ShapeDtypeStruct((n, 8, TOK_DEV), f32),
            jax.ShapeDtypeStruct((n_dp, *blocks), bf16),
        ),
        in_specs=[
            pl.BlockSpec((nb, 2, TOK_DEV, rank), lambda i: (i, 0, 0, 0)),
            pl.BlockSpec((nb * TOK_DEV, 8), lambda i: (i, 0)),
            whole(proj_in),
            whole(gate_factor),
            whole(up_factor),
            whole(down_factor),
            whole(proj_out),
        ],
        out_specs=(
            pl.BlockSpec((nb, 2, TOK_DEV, rank), lambda i: (i, 0, 0, 0)),
            pl.BlockSpec((nb, 8, TOK_DEV), lambda i: (i, 0, 0)),
            pl.BlockSpec((n_dp, *blocks), lambda i: (0, 0, 0, 0, 0)),
        ),
        scratch_shapes=[pltpu.VMEM((EXP_DEV, LANES, 3 * ff + 2 * rank), f32)],
        compiler_params=pltpu.CompilerParams(vmem_limit_bytes=VMEM_LIMIT),
        name="experts",
    )(x, w_rows, proj_in, gate_factor, up_factor, down_factor, proj_out)

    rows_b = width // n
    grad_input, grad_basis, grads, route_got = pl.pallas_call(
        functools.partial(combine_kernel, n, n_dp),
        out_shape=(
            jax.ShapeDtypeStruct((TOK_DEV, model), bf16),
            jax.ShapeDtypeStruct((rows_b, rank), f32),
            jax.ShapeDtypeStruct(blocks, f32),
            jax.ShapeDtypeStruct((n, 8, TOK_DEV), f32),
        ),
        in_specs=[vmem] * 5,
        out_specs=(vmem,) * 4,
        scratch_shapes=[
            pltpu.VMEM((nz, 2, TOK_DEV, rank), bf16),
            pltpu.VMEM((nz, 2, TOK_DEV, rank), bf16),
            pltpu.VMEM((2, TOK_DEV, rank), f32),
            pltpu.VMEM((n_dp, 2, TOK_DEV, rank), bf16),
            pltpu.VMEM((n, rows_b, rank), bf16),
            pltpu.VMEM((nz, rows_b, rank), bf16),
            pltpu.VMEM((nz, rows_b, rank), bf16),
            pltpu.VMEM((n_dp, *blocks), bf16),
            dma((n_dp,)),
            dma((n_dp,)),
            dma((n,)),
            dma((n,)),
            dma((nz,)),
            dma((nz,)),
            dma((nz,)),
            dma((nz,)),
            dma((n_dp,)),
            dma((n_dp,)),
            dma((nz,)),
            dma((nz,)),
            dma((nz,)),
            dma((nz,)),
        ],
        compiler_params=pltpu.CompilerParams(
            collective_id=1, has_side_effects=True, vmem_limit_bytes=VMEM_LIMIT
        ),
        name="combine",
    )(part, route, packed, cols, basis)

    dots = route_got[:, :EXP_DEV].reshape(experts, TOK_DEV).T
    grad_route = jnp.sum(jnp.where(chosen, dots[:, :, None], 0.0), axis=1) / route_weights
    deep, wide = rank // n_dp // LANES, ff // n_dp // LANES
    cuts = [0, deep, deep + wide, deep + 2 * wide, deep + 3 * wide, 2 * deep + 3 * wide]
    g = [grads[:, a:b] for a, b in zip(cuts, cuts[1:])]
    across = lambda t: t.transpose(0, 2, 1, 3).reshape(EXP_DEV, LANES, -1)
    along = lambda t: t.transpose(0, 1, 3, 2).reshape(EXP_DEV, -1, LANES)
    return (
        grad_input,
        grad_route,
        grad_basis,
        along(g[0]),
        across(g[1]),
        across(g[2]),
        along(g[3]),
        across(g[4]),
    )


def solution(mesh):
    split = P(("dp", "expert"), None)
    held = P("expert", None, None)
    in_specs = (split, split, P(), split, split, held, held, held, held, held)
    out_specs = (
        split,
        split,
        split,
        P("expert", "dp", None),
        P("expert", None, "dp"),
        P("expert", None, "dp"),
        P("expert", "dp", None),
        P("expert", None, "dp"),
    )
    return jax.shard_map(
        functools.partial(per_device, mesh.shape["expert"], mesh.shape["dp"]),
        mesh=mesh,
        in_specs=in_specs,
        out_specs=out_specs,
        check_vma=False,
    )
```

```python
import functools

import jax
import jax.numpy as jnp
from jax import lax
from jax.experimental import pallas as pl
from jax.experimental.pallas import tpu as pltpu
from jax.sharding import PartitionSpec as P

EXP_DEV = 2
TOK_DEV = 128
LANES = 128
VMEM_LIMIT = 58 * 1024 * 1024
MESH = pl.DeviceIdType.MESH
f32 = jnp.float32
bf16 = jnp.bfloat16


def remote(src, dst, send, recv, **device):
    return pltpu.make_async_remote_copy(
        src_ref=src, dst_ref=dst, send_sem=send, recv_sem=recv, device_id=device, device_id_type=MESH
    )


def dot(a, b):
    return jnp.dot(a, b, preferred_element_type=f32)


def dot_nt(a, b):
    return lax.dot_general(a, b, (((1,), (1,)), ((), ())), preferred_element_type=f32)


def dot_tn(a, b):
    return lax.dot_general(a, b, (((0,), (0,)), ((), ())), preferred_element_type=f32)


def loop(low, high, body):
    def step(i, carry):
        body(i)
        return carry

    lax.fori_loop(low, high, step, 0)


def greet(n, n_dp, me, p):
    barrier = pltpu.get_barrier_semaphore()

    def expert_peer(d):
        pl.semaphore_signal(
            barrier, inc=1, device_id={"expert": lax.rem(me + d, n)}, device_id_type=MESH
        )

    def dp_peer(d):
        pl.semaphore_signal(
            barrier, inc=1, device_id={"dp": lax.rem(p + d, n_dp)}, device_id_type=MESH
        )

    loop(1, n, expert_peer)
    loop(1, n_dp, dp_peer)
    pl.semaphore_wait(barrier, n - 1 + n_dp - 1)


def gather_kernel(
    n, n_dp, act, cot, basis, wt, x_out, w_out, cols_out, s_c, r_c, s_x, r_x, s_f, s_w, r_w
):
    me, p = lax.axis_index("expert"), lax.axis_index("dp")
    nz = n // 2
    core, z = lax.rem(me, 2), me // 2
    sib = me + 1 - 2 * core
    width = act.shape[1] // n_dp
    greet(n, n_dp, me, p)

    def w_copy(d):
        return remote(
            wt.at[lax.rem(me + d, n)], w_out.at[me], s_w.at[d], r_w.at[me], expert=lax.rem(me + d, n)
        )

    loop(1, n, lambda d: w_copy(d).start())

    def x_copy(a, d, to):
        return remote(x_out.at[me, a], x_out.at[me, a], s_x.at[a, d], r_x.at[a, me], expert=to)

    def line_peer(d):
        return lax.rem(z + d, nz) * 2 + core

    for a, ref in enumerate((act, cot)):
        x_out[me, a] = dot(ref[...], basis[...]).astype(bf16)
        loop(1, nz, lambda d: x_copy(a, d, line_peer(d)).start())
        x_copy(a, 0, sib).start()

    def col_copy(a, d):
        q = lax.rem(p + d, n_dp)
        ref = (act, cot)[a]
        return remote(
            ref.at[:, pl.ds(pl.multiple_of(q * width, LANES), width)],
            cols_out.at[p, a],
            s_c.at[a, d],
            r_c.at[a, p],
            dp=q,
        )

    for a in range(2):
        loop(1, n_dp, lambda d: col_copy(a, d).start())
    for a, ref in enumerate((act, cot)):
        cols_out[p, a] = ref[:, pl.ds(pl.multiple_of(p * width, LANES), width)]
    w_out[me] = wt[me]

    def forward(a, d):
        src = lax.rem(z + nz - d, nz) * 2 + core
        return remote(x_out.at[src, a], x_out.at[src, a], s_f.at[a, d], r_x.at[a, src], expert=sib)

    def pass_on(a, d):
        forward(a, d).wait_recv()
        forward(a, d).start()

    for a in range(2):
        loop(1, nz, lambda d: pass_on(a, d))

    def sib_wait(a, k):
        src = k * 2 + 1 - core
        remote(
            x_out.at[src, a], x_out.at[src, a], s_f.at[a, 0], r_x.at[a, src], expert=sib
        ).wait_recv()

    def w_wait(d):
        src = lax.rem(me + n - d, n)
        remote(wt.at[src], w_out.at[src], s_w.at[d], r_w.at[src], expert=src).wait_recv()

    def col_wait(a, d):
        src = lax.rem(p + n_dp - d, n_dp)
        remote(cols_out.at[src, a], cols_out.at[src, a], s_c.at[a, d], r_c.at[a, src], dp=src).wait_recv()

    loop(1, n, w_wait)
    for a in range(2):
        loop(0, nz, lambda k: sib_wait(a, k))
        loop(1, n_dp, lambda d: col_wait(a, d))
    loop(1, n, lambda d: w_copy(d).wait_send())
    for a in range(2):
        x_copy(a, 0, sib).wait_send()
        loop(1, nz, lambda d: x_copy(a, d, line_peer(d)).wait_send())
        loop(1, nz, lambda d: forward(a, d).wait_send())
        loop(1, n_dp, lambda d: col_copy(a, d).wait_send())


def expert_rows(e, chunk, coords, back, we, pin, gate, up, down, pout, acc):
    rows, rank = back.shape
    ff = gate.shape[2]
    scaled = (we * back).astype(bf16)
    codes = dot(coords, pin[e]).astype(bf16)
    d_narrow32 = dot_nt(scaled, pout[e])
    d_narrow = d_narrow32.astype(bf16)
    codes_t, d_narrow_t = codes.T, d_narrow.T
    narrow32 = jnp.zeros((rows, LANES), f32)
    d_codes32 = jnp.zeros((rows, LANES), f32)
    for at in range(0, ff, chunk):
        now = slice(at, at + chunk)
        gate_pre = dot(codes, gate[e, :, now])
        up_pre = dot(codes, up[e, :, now])
        d_hidden = dot_nt(d_narrow, down[e, now, :])
        sig = 0.5 * jnp.tanh(0.5 * gate_pre) + 0.5
        active = gate_pre * sig
        slope = sig + active * (1.0 - sig)
        hidden = (active * up_pre).astype(bf16)
        d_gate = (d_hidden * up_pre * slope).astype(bf16)
        d_up = (d_hidden * active).astype(bf16)
        narrow32 += dot(hidden, down[e, now, :])
        d_codes32 += dot_nt(d_gate, gate[e, :, now]) + dot_nt(d_up, up[e, :, now])
        acc[e, :, at : at + chunk] += dot(codes_t, d_gate)
        acc[e, :, ff + at : ff + at + chunk] += dot(codes_t, d_up)
        acc[e, :, 2 * ff + at : 2 * ff + at + chunk] += dot(d_narrow_t, hidden)
    narrow = narrow32.astype(bf16)
    d_codes = d_codes32.astype(bf16)
    outcome = dot(narrow, pout[e]).astype(bf16)
    acc[e, :, 3 * ff : 3 * ff + rank] += dot(d_codes.T, coords)
    acc[e, :, 3 * ff + rank :] += dot(narrow.T, scaled)
    sums = lax.dot_general(
        jnp.ones((8, LANES), f32),
        narrow.astype(f32) * d_narrow32,
        (((1,), (1,)), ((), ())),
        precision=lax.Precision.HIGHEST,
        preferred_element_type=f32,
    )
    return we * outcome.astype(f32), dot_nt(d_codes, pin[e]), sums


def pack(n_dp, ff, rank, e, acc, packed):
    wide, deep = ff // n_dp, rank // n_dp
    for q in range(n_dp):
        starts = [3 * ff + q * deep + i for i in range(0, deep, LANES)]
        for base in (0, ff, 2 * ff):
            starts += [base + q * wide + i for i in range(0, wide, LANES)]
        starts += [3 * ff + rank + q * deep + i for i in range(0, deep, LANES)]
        for i, at in enumerate(starts):
            packed[q, e, i] = acc[e, :, at : at + LANES].astype(bf16)


def expert_kernel(n_dp, chunk, x, w, pin, gate, up, down, pout, part, route, packed, acc):
    step = pl.program_id(0)
    nb, rank = x.shape[0], x.shape[3]
    rows = nb * TOK_DEV
    ff = gate.shape[2]

    @pl.when(step == 0)
    def _():
        acc[...] = jnp.zeros_like(acc)

    coords = x[:, 0].reshape(rows, rank)
    back = x[:, 1].reshape(rows, rank).astype(f32)
    dz = jnp.zeros((rows, rank), f32)
    mixed = jnp.zeros((rows, rank), f32)
    dots = jnp.zeros((8, rows), f32)
    line = lax.broadcasted_iota(jnp.int32, (8, rows), 0)
    for e in range(EXP_DEV):
        m, g, sums = expert_rows(
            e, chunk, coords, back, w[:, e : e + 1], pin, gate, up, down, pout, acc
        )
        mixed += m
        dz += g
        dots = jnp.where(line == e, sums, dots)
    part[:, 0] = dz.astype(bf16).reshape(nb, TOK_DEV, rank)
    part[:, 1] = mixed.astype(bf16).reshape(nb, TOK_DEV, rank)
    for b in range(nb):
        route[b] = dots[:, b * TOK_DEV : (b + 1) * TOK_DEV]

    @pl.when(step == pl.num_programs(0) - 1)
    def _():
        for e in range(EXP_DEV):
            pack(n_dp, ff, rank, e, acc, packed)


def expert_sum(n, me, part, held, landed, total, s1, r1, s2, r2):
    nz = n // 2
    core, z = lax.rem(me, 2), me // 2
    sib = me + 1 - 2 * core

    def to_sib(k):
        return remote(part.at[k * 2 + 1 - core], held.at[k], s1.at[k], r1.at[k], expert=sib)

    def to_line(d):
        k = lax.rem(z + d, nz)
        return remote(held.at[k], landed.at[z], s2.at[d], r2.at[z], expert=k * 2 + core)

    loop(1, nz, lambda d: to_sib(lax.rem(z + d, nz)).start())
    to_sib(z).start()

    def add(d):
        k = lax.rem(z + d, nz)
        to_sib(k).wait_recv()
        held[k] = (part[k * 2 + core].astype(f32) + held[k].astype(f32)).astype(bf16)
        to_line(d).start()

    loop(1, nz, add)
    to_sib(z).wait_recv()
    total[...] = part[me].astype(f32) + held[z].astype(f32)

    def collect(d):
        k = lax.rem(z + nz - d, nz)
        remote(held.at[k], landed.at[k], s2.at[d], r2.at[k], expert=k * 2 + core).wait_recv()
        total[...] += landed[k].astype(f32)

    loop(1, nz, collect)
    loop(0, nz, lambda k: to_sib(k).wait_send())
    loop(1, nz, lambda d: to_line(d).wait_send())


def combine_kernel(
    n,
    n_dp,
    part,
    route,
    packed,
    cols,
    basis,
    grad_input,
    grad_basis,
    grads,
    route_out,
    held,
    landed,
    total,
    dzm,
    block,
    held_b,
    landed_b,
    grads_in,
    s_g,
    r_g,
    s_r,
    r_r,
    s1,
    r1,
    s2,
    r2,
    s_d,
    r_d,
    t1,
    q1,
    t2,
    q2,
):
    me, p = lax.axis_index("expert"), lax.axis_index("dp")
    rank = basis.shape[1]
    greet(n, n_dp, me, p)

    def route_copy(d):
        j = lax.rem(me + d, n)
        return remote(route.at[j], route_out.at[me], s_r.at[d], r_r.at[me], expert=j)

    def grad_copy(d):
        q = lax.rem(p + d, n_dp)
        return remote(packed.at[q], grads_in.at[p], s_g.at[d], r_g.at[p], dp=q)

    loop(1, n, lambda d: route_copy(d).start())
    loop(1, n_dp, lambda d: grad_copy(d).start())
    route_out[me] = route[me]
    expert_sum(n, me, part, held, landed, total, s1, r1, s2, r2)
    dzm[p] = total[...].astype(bf16)

    def dzm_copy(d):
        q = lax.rem(p + d, n_dp)
        return remote(dzm.at[p], dzm.at[p], s_d.at[d], r_d.at[p], dp=q)

    loop(1, n_dp, lambda d: dzm_copy(d).start())
    grad_input[...] = dot_nt(dzm[p, 0], basis[...]).astype(bf16)

    def dzm_wait(d):
        src = lax.rem(p + n_dp - d, n_dp)
        remote(dzm.at[src], dzm.at[src], s_d.at[d], r_d.at[src], dp=src).wait_recv()

    loop(1, n_dp, dzm_wait)
    tokens = n_dp * 2 * TOK_DEV
    width = cols.shape[3]
    sums = dot_tn(cols[...].reshape(tokens, width), dzm[...].reshape(tokens, rank))
    block[...] = sums.astype(bf16).reshape(block.shape)
    expert_sum(n, me, block, held_b, landed_b, grad_basis, t1, q1, t2, q2)

    def grad_wait(d):
        src = lax.rem(p + n_dp - d, n_dp)
        remote(grads_in.at[src], grads_in.at[src], s_g.at[d], r_g.at[src], dp=src).wait_recv()
        grads[...] += grads_in[src].astype(f32)

    grads[...] = packed[p].astype(f32)
    loop(1, n_dp, grad_wait)

    def route_wait(d):
        src = lax.rem(me + n - d, n)
        remote(route.at[src], route_out.at[src], s_r.at[d], r_r.at[src], expert=src).wait_recv()

    loop(1, n, route_wait)
    loop(1, n, lambda d: route_copy(d).wait_send())
    loop(1, n_dp, lambda d: grad_copy(d).wait_send())
    loop(1, n_dp, lambda d: dzm_copy(d).wait_send())


def crossed(z, d, nz):
    k, bit = 0, 1
    while bit < nz:
        zb, db = lax.rem(z // bit, 2), lax.rem(d // bit, 2)
        k = k + bit * (zb + db - 2 * zb * db)
        bit *= 2
    return k


def layer_kernel(
    n, n_dp, chunk,
    act_h, cot_h, basis_h, wt, pin_h, pout_h, gate_h, up_h, down_h,
    grad_input, grad_basis, grads, route_out,
    act, cot, basis, pin, pout, gate, up, down,
    x, w_in, cols, cols_t, acc, part, route, packed, grads_in,
    held, landed, total, dzm, block, held_b, landed_b,
    s_l, s_c, r_c, s_x, r_x, s_f, s_w, r_w, s_g, r_g, s_r, r_r,
    s1, r1, s2, r2, s_d, r_d, t1, q1, t2, q2,
):
    me, p = lax.axis_index("expert"), lax.axis_index("dp")
    nz = n // 2
    core, z = lax.rem(me, 2), me // 2
    sib = me + 1 - 2 * core
    rank = basis.shape[1]
    ff = gate.shape[2]
    width = act.shape[1] // n_dp
    rows = 2 * TOK_DEV

    loads = [
        pltpu.make_async_copy(src, dst, s_l.at[i])
        for i, (src, dst) in enumerate(
            zip(
                (act_h, basis_h, cot_h, pin_h, pout_h, gate_h, up_h, down_h),
                (act, basis, cot, pin, pout, gate, up, down),
            )
        )
    ]
    for load in loads:
        load.start()
    greet(n, n_dp, me, p)

    def w_copy(d):
        j = lax.rem(me + d, n)
        return remote(wt.at[j], w_in.at[me], s_w.at[d], r_w.at[me], expert=j)

    loop(1, n, lambda d: w_copy(d).start())

    def peer(d):
        return crossed(z, d, nz)

    def x_copy(a, d, to):
        return remote(x.at[me, a], x.at[me, a], s_x.at[a, d], r_x.at[a, me], expert=to)

    loads[0].wait()
    loads[1].wait()
    for a, ref in enumerate((act, cot)):
        if a == 1:
            loads[2].wait()
        x[me, a] = dot(ref[...], basis[...]).astype(bf16)
        x_copy(a, 0, sib).start()
        loop(1, nz, lambda d: x_copy(a, d, peer(d) * 2 + core).start())

    def col_copy(a, d):
        q = lax.rem(p + d, n_dp)
        return remote(
            (act, cot)[a].at[:, pl.ds(pl.multiple_of(q * width, LANES), width)],
            cols.at[p, a],
            s_c.at[a, d],
            r_c.at[a, p],
            dp=q,
        )

    for a in range(2):
        loop(1, n_dp, lambda d: col_copy(a, d).start())
    for a, ref in enumerate((act, cot)):
        cols[p, a] = ref[:, pl.ds(pl.multiple_of(p * width, LANES), width)]
    w_in[me] = wt[me]
    acc[...] = jnp.zeros_like(acc)

    def w_wait(d):
        src = lax.rem(me + n - d, n)
        remote(wt.at[src], w_in.at[src], s_w.at[d], r_w.at[src], expert=src).wait_recv()

    loop(1, n, w_wait)
    for load in loads[3:]:
        load.wait()

    def forward(a, d):
        src = peer(d) * 2 + core
        return remote(x.at[src, a], x.at[src, a], s_f.at[a, d], r_x.at[a, src], expert=sib)

    def from_sib(a, d):
        src = peer(d) * 2 + 1 - core
        return remote(x.at[src, a], x.at[src, a], s_f.at[a, d], r_x.at[a, src], expert=sib)

    def to_sib(k):
        return remote(part.at[k * 2 + 1 - core], held.at[k], s1.at[k], r1.at[k], expert=sib)

    def to_line(d):
        k = peer(d)
        return remote(held.at[k], landed.at[z], s2.at[d], r2.at[z], expert=k * 2 + core)

    def combine(d):
        k = peer(d)
        to_sib(k).wait_recv()
        held[k] = (part[k * 2 + core].astype(f32) + held[k].astype(f32)).astype(bf16)
        to_line(d).start()

    def grad_copy(e, d):
        q = lax.rem(p + d, n_dp)
        return remote(packed.at[q, e], grads_in.at[p, e], s_g.at[e, d], r_g.at[e, p], dp=q)

    def send_grads(e):
        pack(n_dp, ff, rank, e, acc, packed)
        loop(1, n_dp, lambda d: grad_copy(e, d).start())

    line = lax.broadcasted_iota(jnp.int32, (8, rows), 0)
    square = (TOK_DEV, TOK_DEV)
    eye = lax.broadcasted_iota(jnp.int32, square, 0) == lax.broadcasted_iota(jnp.int32, square, 1)

    def pair(d):
        k = peer(d)

        @pl.when(d > 0)
        def _():
            for a in range(2):
                forward(a, d).wait_recv()
                forward(a, d).start()

        for a in range(2):
            from_sib(a, d).wait_recv()
        both = pl.ds(k * 2, 2)
        coords = x[both, 0].reshape(rows, rank)
        back = x[both, 1].reshape(rows, rank).astype(f32)

        def column(e):
            return jnp.concatenate(
                [
                    jnp.sum(jnp.where(eye, w_in[k * 2 + b, e : e + 1, :], 0.0), axis=1, keepdims=True)
                    for b in range(2)
                ],
                axis=0,
            )

        @pl.when(d > 1)
        def _():
            combine(d - 1)

        mixed = jnp.zeros((rows, rank), f32)
        dz = jnp.zeros((rows, rank), f32)
        dots = jnp.zeros((8, rows), f32)
        for e in range(EXP_DEV):
            m, g, sums = expert_rows(
                e, chunk, coords, back, column(e), pin, gate, up, down, pout, acc
            )
            mixed += m
            dz += g
            dots = jnp.where(line == e, sums, dots)
        part[both, 0] = dz.astype(bf16).reshape(2, TOK_DEV, rank)
        part[both, 1] = mixed.astype(bf16).reshape(2, TOK_DEV, rank)
        for b in range(2):
            route[k * 2 + b] = dots[:, b * TOK_DEV : (b + 1) * TOK_DEV]
        to_sib(k).start()

    loop(0, nz, pair)
    send_grads(0)
    if nz > 1:
        combine(nz - 1)

    def route_copy(d):
        j = lax.rem(me + d, n)
        return remote(route.at[j], route_out.at[me], s_r.at[d], r_r.at[me], expert=j)

    loop(1, n, lambda d: route_copy(d).start())
    route_out[me] = route[me]
    for e in range(1, EXP_DEV):
        pack(n_dp, ff, rank, e, acc, packed)
    to_sib(z).wait_recv()
    total[...] = part[me].astype(f32) + held[z].astype(f32)

    def collect(d):
        k = peer(d)
        remote(held.at[k], landed.at[k], s2.at[d], r2.at[k], expert=k * 2 + core).wait_recv()
        total[...] += landed[k].astype(f32)

    loop(1, nz, collect)
    dzm[p] = total[...].astype(bf16)

    def dzm_copy(d):
        q = lax.rem(p + d, n_dp)
        return remote(dzm.at[p], dzm.at[p], s_d.at[d], r_d.at[p], dp=q)

    loop(1, n_dp, lambda d: dzm_copy(d).start())
    for e in range(1, EXP_DEV):
        loop(1, n_dp, lambda d: grad_copy(e, d).start())

    def col_wait(a, d):
        src = lax.rem(p + n_dp - d, n_dp)
        remote(cols.at[src, a], cols.at[src, a], s_c.at[a, d], r_c.at[a, src], dp=src).wait_recv()

    for a in range(2):
        loop(1, n_dp, lambda d: col_wait(a, d))
    for q in range(n_dp):
        for a in range(2):
            at = (q * 2 + a) * TOK_DEV
            cols_t[:, at : at + TOK_DEV] = cols[q, a].T
    grad_input[...] = dot_nt(dzm[p, 0], basis[...]).astype(bf16)

    def dzm_wait(d):
        src = lax.rem(p + n_dp - d, n_dp)
        remote(dzm.at[src], dzm.at[src], s_d.at[d], r_d.at[src], dp=src).wait_recv()

    loop(1, n_dp, dzm_wait)
    sums = dot(cols_t[...], dzm[...].reshape(n_dp * rows, rank))
    block[...] = sums.astype(bf16).reshape(block.shape)
    expert_sum(n, me, block, held_b, landed_b, grad_basis, t1, q1, t2, q2)

    def grad_wait(e, d):
        src = lax.rem(p + n_dp - d, n_dp)
        remote(
            grads_in.at[src, e], grads_in.at[src, e], s_g.at[e, d], r_g.at[e, src], dp=src
        ).wait_recv()
        grads[e] += grads_in[src, e].astype(f32)

    for e in range(EXP_DEV):
        grads[e] = packed[p, e].astype(f32)
        loop(1, n_dp, lambda d: grad_wait(e, d))

    def route_wait(d):
        src = lax.rem(me + n - d, n)
        remote(route.at[src], route_out.at[src], s_r.at[d], r_r.at[src], expert=src).wait_recv()

    loop(1, n, route_wait)
    loop(1, n, lambda d: route_copy(d).wait_send())
    loop(1, n, lambda d: w_copy(d).wait_send())
    for a in range(2):
        x_copy(a, 0, sib).wait_send()
        loop(1, nz, lambda d: x_copy(a, d, peer(d) * 2 + core).wait_send())
        loop(1, nz, lambda d: forward(a, d).wait_send())
        loop(1, n_dp, lambda d: col_copy(a, d).wait_send())
    loop(0, nz, lambda k: to_sib(k).wait_send())
    loop(1, nz, lambda d: to_line(d).wait_send())
    loop(1, n_dp, lambda d: dzm_copy(d).wait_send())
    for e in range(EXP_DEV):
        loop(1, n_dp, lambda d: grad_copy(e, d).wait_send())


def finish_kernel(
    gi, gb, grads, grad_input, grad_basis, g_in, g_gate, g_up, g_down, g_out,
):
    grad_input[...] = gi[...]
    grad_basis[...] = gb[...]
    deep, wide = g_in.shape[1] // LANES, g_gate.shape[2] // LANES
    for e in range(EXP_DEV):
        for i in range(deep):
            at = slice(i * LANES, (i + 1) * LANES)
            g_in[e, at, :] = grads[e, i].T
            g_out[e, :, at] = grads[e, deep + 3 * wide + i]
        for i in range(wide):
            at = slice(i * LANES, (i + 1) * LANES)
            g_gate[e, :, at] = grads[e, deep + i]
            g_up[e, :, at] = grads[e, deep + wide + i]
            g_down[e, at, :] = grads[e, deep + 2 * wide + i].T


def whole_layer(n, n_dp, shapes, blocks, arrays, wt):
    model, rank, ff = shapes
    nz = n // 2
    width = model // n_dp
    rows_b = width // n
    vmem = pl.BlockSpec(memory_space=pltpu.VMEM)
    hbm = pl.BlockSpec(memory_space=pl.ANY)
    dma = pltpu.SemaphoreType.DMA
    act, cot, basis, *weights = arrays
    token = (TOK_DEV, rank)
    return pl.pallas_call(
        functools.partial(layer_kernel, n, n_dp, ff // 3),
        out_shape=(
            jax.ShapeDtypeStruct((TOK_DEV, model), bf16),
            jax.ShapeDtypeStruct((rows_b, rank), f32),
            jax.ShapeDtypeStruct(blocks, f32),
            jax.ShapeDtypeStruct((n, 8, TOK_DEV), f32),
        ),
        in_specs=[hbm] * 3 + [vmem] + [hbm] * 5,
        out_specs=(vmem,) * 4,
        scratch_shapes=[pltpu.VMEM(a.shape, bf16) for a in arrays]
        + [
            pltpu.VMEM((n, 2, *token), bf16),
            pltpu.VMEM((n, 8, TOK_DEV), f32),
            pltpu.VMEM((n_dp, 2, TOK_DEV, width), bf16),
            pltpu.VMEM((width, n_dp * 2 * TOK_DEV), bf16),
            pltpu.VMEM((EXP_DEV, LANES, 3 * ff + 2 * rank), f32),
            pltpu.VMEM((n, 2, *token), bf16),
            pltpu.VMEM((n, 8, TOK_DEV), f32),
            pltpu.VMEM((n_dp, *blocks), bf16),
            pltpu.VMEM((n_dp, *blocks), bf16),
            pltpu.VMEM((nz, 2, *token), bf16),
            pltpu.VMEM((nz, 2, *token), bf16),
            pltpu.VMEM((2, *token), f32),
            pltpu.VMEM((n_dp, 2, *token), bf16),
            pltpu.VMEM((n, rows_b, rank), bf16),
            pltpu.VMEM((nz, rows_b, rank), bf16),
            pltpu.VMEM((nz, rows_b, rank), bf16),
        ]
        + [
            dma(s)
            for s in (
                (8,), (2, n_dp), (2, n_dp), (2, nz), (2, n), (2, nz), (n,), (n,),
                (EXP_DEV, n_dp), (EXP_DEV, n_dp), (n,), (n,),
                (nz,), (nz,), (nz,), (nz,), (n_dp,), (n_dp,), (nz,), (nz,), (nz,), (nz,),
            )
        ],
        compiler_params=pltpu.CompilerParams(
            collective_id=2, has_side_effects=True, vmem_limit_bytes=VMEM_LIMIT
        ),
        name="whole_layer",
    )(act, cot, basis, wt, *weights)


def staged_layer(n, n_dp, shapes, blocks, arrays, wt):
    model, rank, ff = shapes
    nz = n // 2
    width = model // n_dp
    vmem = pl.BlockSpec(memory_space=pltpu.VMEM)
    dma = pltpu.SemaphoreType.DMA
    activations, cotangent, basis, proj_in, proj_out, gate_factor, up_factor, down_factor = arrays
    x, w_all, cols = pl.pallas_call(
        functools.partial(gather_kernel, n, n_dp),
        out_shape=(
            jax.ShapeDtypeStruct((n, 2, TOK_DEV, rank), bf16),
            jax.ShapeDtypeStruct((n, 8, TOK_DEV), f32),
            jax.ShapeDtypeStruct((n_dp, 2, TOK_DEV, width), bf16),
        ),
        in_specs=[vmem] * 4,
        out_specs=(vmem,) * 3,
        scratch_shapes=[
            dma((2, n_dp)),
            dma((2, n_dp)),
            dma((2, nz)),
            dma((2, n)),
            dma((2, nz)),
            dma((n,)),
            dma((n,)),
        ],
        compiler_params=pltpu.CompilerParams(
            collective_id=0, has_side_effects=True, vmem_limit_bytes=VMEM_LIMIT
        ),
        name="gather_tokens",
    )(activations, cotangent, basis, wt)

    w_rows = w_all.transpose(0, 2, 1).reshape(n * TOK_DEV, 8)
    nb = 2
    whole = lambda a: pl.BlockSpec(a.shape, lambda i: (0,) * a.ndim)
    part, route, packed = pl.pallas_call(
        functools.partial(expert_kernel, n_dp, ff // 3),
        grid=(n // nb,),
        out_shape=(
            jax.ShapeDtypeStruct((n, 2, TOK_DEV, rank), bf16),
            jax.ShapeDtypeStruct((n, 8, TOK_DEV), f32),
            jax.ShapeDtypeStruct((n_dp, *blocks), bf16),
        ),
        in_specs=[
            pl.BlockSpec((nb, 2, TOK_DEV, rank), lambda i: (i, 0, 0, 0)),
            pl.BlockSpec((nb * TOK_DEV, 8), lambda i: (i, 0)),
            whole(proj_in),
            whole(gate_factor),
            whole(up_factor),
            whole(down_factor),
            whole(proj_out),
        ],
        out_specs=(
            pl.BlockSpec((nb, 2, TOK_DEV, rank), lambda i: (i, 0, 0, 0)),
            pl.BlockSpec((nb, 8, TOK_DEV), lambda i: (i, 0, 0)),
            pl.BlockSpec((n_dp, *blocks), lambda i: (0, 0, 0, 0, 0)),
        ),
        scratch_shapes=[pltpu.VMEM((EXP_DEV, LANES, 3 * ff + 2 * rank), f32)],
        compiler_params=pltpu.CompilerParams(vmem_limit_bytes=VMEM_LIMIT),
        name="experts",
    )(x, w_rows, proj_in, gate_factor, up_factor, down_factor, proj_out)

    rows_b = width // n
    return pl.pallas_call(
        functools.partial(combine_kernel, n, n_dp),
        out_shape=(
            jax.ShapeDtypeStruct((TOK_DEV, model), bf16),
            jax.ShapeDtypeStruct((rows_b, rank), f32),
            jax.ShapeDtypeStruct(blocks, f32),
            jax.ShapeDtypeStruct((n, 8, TOK_DEV), f32),
        ),
        in_specs=[vmem] * 5,
        out_specs=(vmem,) * 4,
        scratch_shapes=[
            pltpu.VMEM((nz, 2, TOK_DEV, rank), bf16),
            pltpu.VMEM((nz, 2, TOK_DEV, rank), bf16),
            pltpu.VMEM((2, TOK_DEV, rank), f32),
            pltpu.VMEM((n_dp, 2, TOK_DEV, rank), bf16),
            pltpu.VMEM((n, rows_b, rank), bf16),
            pltpu.VMEM((nz, rows_b, rank), bf16),
            pltpu.VMEM((nz, rows_b, rank), bf16),
            pltpu.VMEM((n_dp, *blocks), bf16),
            dma((n_dp,)),
            dma((n_dp,)),
            dma((n,)),
            dma((n,)),
            dma((nz,)),
            dma((nz,)),
            dma((nz,)),
            dma((nz,)),
            dma((n_dp,)),
            dma((n_dp,)),
            dma((nz,)),
            dma((nz,)),
            dma((nz,)),
            dma((nz,)),
        ],
        compiler_params=pltpu.CompilerParams(
            collective_id=1, has_side_effects=True, vmem_limit_bytes=VMEM_LIMIT
        ),
        name="combine",
    )(part, route, packed, cols, basis)


def per_device(
    n,
    n_dp,
    activations,
    cotangent,
    basis,
    route_ids,
    route_weights,
    proj_in,
    gate_factor,
    up_factor,
    down_factor,
    proj_out,
):
    model, rank = basis.shape
    ff = gate_factor.shape[2]
    experts = EXP_DEV * n

    chosen = route_ids[:, None, :] == jnp.arange(experts, dtype=jnp.int32)[None, :, None]
    dense = jnp.sum(jnp.where(chosen, route_weights[:, None, :], 0.0), axis=2)
    wt = dense.T.reshape(n, EXP_DEV, TOK_DEV)
    wt = jnp.pad(wt, ((0, 0), (0, 8 - EXP_DEV), (0, 0)))

    blocks = EXP_DEV, (2 * rank + 3 * ff) // n_dp // LANES, LANES, LANES
    arrays = activations, cotangent, basis, proj_in, proj_out, gate_factor, up_factor, down_factor
    tokens = n * TOK_DEV * rank * 2
    fits = 6 * tokens + 34 * 1024 * 1024 < VMEM_LIMIT and (n & (n - 1)) == 0
    layer = whole_layer if fits else staged_layer
    grad_input, grad_basis, grads, dots = layer(n, n_dp, (model, rank, ff), blocks, arrays, wt)
    deep, wide = rank // n_dp, ff // n_dp
    vmem = pl.BlockSpec(memory_space=pltpu.VMEM)
    grad_input, grad_basis, *factors = pl.pallas_call(
        finish_kernel,
        out_shape=(
            jax.ShapeDtypeStruct(grad_input.shape, bf16),
            jax.ShapeDtypeStruct(grad_basis.shape, f32),
            jax.ShapeDtypeStruct((EXP_DEV, deep, LANES), f32),
            jax.ShapeDtypeStruct((EXP_DEV, LANES, wide), f32),
            jax.ShapeDtypeStruct((EXP_DEV, LANES, wide), f32),
            jax.ShapeDtypeStruct((EXP_DEV, wide, LANES), f32),
            jax.ShapeDtypeStruct((EXP_DEV, LANES, deep), f32),
        ),
        in_specs=[vmem] * 3,
        out_specs=(vmem,) * 7,
        compiler_params=pltpu.CompilerParams(vmem_limit_bytes=VMEM_LIMIT),
        name="finish",
    )(grad_input, grad_basis, grads)
    dots = dots[:, :EXP_DEV].reshape(experts, TOK_DEV).T
    grad_route = jnp.sum(jnp.where(chosen, dots[:, :, None], 0.0), axis=1) / route_weights
    return (grad_input, grad_route, grad_basis, *factors)


def solution(mesh):
    split = P(("dp", "expert"), None)
    held = P("expert", None, None)
    in_specs = (split, split, P(), split, split, held, held, held, held, held)
    out_specs = (
        split,
        split,
        split,
        P("expert", "dp", None),
        P("expert", None, "dp"),
        P("expert", None, "dp"),
        P("expert", "dp", None),
        P("expert", None, "dp"),
    )
    return jax.shard_map(
        functools.partial(per_device, mesh.shape["expert"], mesh.shape["dp"]),
        mesh=mesh,
        in_specs=in_specs,
        out_specs=out_specs,
        check_vma=False,
    )
```

```python
import functools

import jax
import jax.numpy as jnp
from jax import lax
from jax.experimental import pallas as pl
from jax.experimental.pallas import tpu as pltpu
from jax.sharding import PartitionSpec as P

EXP_DEV = 2
TOK_DEV = 128
LANES = 128
VMEM_LIMIT = 58 * 1024 * 1024
MESH = pl.DeviceIdType.MESH
f32 = jnp.float32
bf16 = jnp.bfloat16


def remote(src, dst, send, recv, **device):
    return pltpu.make_async_remote_copy(
        src_ref=src, dst_ref=dst, send_sem=send, recv_sem=recv, device_id=device, device_id_type=MESH
    )


def dot(a, b):
    return jnp.dot(a, b, preferred_element_type=f32)


def dot_nt(a, b):
    return lax.dot_general(a, b, (((1,), (1,)), ((), ())), preferred_element_type=f32)


def dot_tn(a, b):
    return lax.dot_general(a, b, (((0,), (0,)), ((), ())), preferred_element_type=f32)


def loop(low, high, body):
    def step(i, carry):
        body(i)
        return carry

    lax.fori_loop(low, high, step, 0)


def greet(n, n_dp, me, p):
    barrier = pltpu.get_barrier_semaphore()

    def expert_peer(d):
        pl.semaphore_signal(
            barrier, inc=1, device_id={"expert": lax.rem(me + d, n)}, device_id_type=MESH
        )

    def dp_peer(d):
        pl.semaphore_signal(
            barrier, inc=1, device_id={"dp": lax.rem(p + d, n_dp)}, device_id_type=MESH
        )

    loop(1, n, expert_peer)
    loop(1, n_dp, dp_peer)
    pl.semaphore_wait(barrier, n - 1 + n_dp - 1)


def gather_kernel(
    n, n_dp, act, cot, basis, wt, x_out, w_out, cols_out, s_c, r_c, s_x, r_x, s_f, s_w, r_w
):
    me, p = lax.axis_index("expert"), lax.axis_index("dp")
    nz = n // 2
    core, z = lax.rem(me, 2), me // 2
    sib = me + 1 - 2 * core
    width = act.shape[1] // n_dp
    greet(n, n_dp, me, p)

    def w_copy(d):
        return remote(
            wt.at[lax.rem(me + d, n)], w_out.at[me], s_w.at[d], r_w.at[me], expert=lax.rem(me + d, n)
        )

    loop(1, n, lambda d: w_copy(d).start())

    def x_copy(a, d, to):
        return remote(x_out.at[me, a], x_out.at[me, a], s_x.at[a, d], r_x.at[a, me], expert=to)

    def line_peer(d):
        return lax.rem(z + d, nz) * 2 + core

    for a, ref in enumerate((act, cot)):
        x_out[me, a] = dot(ref[...], basis[...]).astype(bf16)
        loop(1, nz, lambda d: x_copy(a, d, line_peer(d)).start())
        x_copy(a, 0, sib).start()

    def col_copy(a, d):
        q = lax.rem(p + d, n_dp)
        ref = (act, cot)[a]
        return remote(
            ref.at[:, pl.ds(pl.multiple_of(q * width, LANES), width)],
            cols_out.at[p, a],
            s_c.at[a, d],
            r_c.at[a, p],
            dp=q,
        )

    for a in range(2):
        loop(1, n_dp, lambda d: col_copy(a, d).start())
    for a, ref in enumerate((act, cot)):
        cols_out[p, a] = ref[:, pl.ds(pl.multiple_of(p * width, LANES), width)]
    w_out[me] = wt[me]

    def forward(a, d):
        src = lax.rem(z + nz - d, nz) * 2 + core
        return remote(x_out.at[src, a], x_out.at[src, a], s_f.at[a, d], r_x.at[a, src], expert=sib)

    def pass_on(a, d):
        forward(a, d).wait_recv()
        forward(a, d).start()

    for a in range(2):
        loop(1, nz, lambda d: pass_on(a, d))

    def sib_wait(a, k):
        src = k * 2 + 1 - core
        remote(
            x_out.at[src, a], x_out.at[src, a], s_f.at[a, 0], r_x.at[a, src], expert=sib
        ).wait_recv()

    def w_wait(d):
        src = lax.rem(me + n - d, n)
        remote(wt.at[src], w_out.at[src], s_w.at[d], r_w.at[src], expert=src).wait_recv()

    def col_wait(a, d):
        src = lax.rem(p + n_dp - d, n_dp)
        remote(cols_out.at[src, a], cols_out.at[src, a], s_c.at[a, d], r_c.at[a, src], dp=src).wait_recv()

    loop(1, n, w_wait)
    for a in range(2):
        loop(0, nz, lambda k: sib_wait(a, k))
        loop(1, n_dp, lambda d: col_wait(a, d))
    loop(1, n, lambda d: w_copy(d).wait_send())
    for a in range(2):
        x_copy(a, 0, sib).wait_send()
        loop(1, nz, lambda d: x_copy(a, d, line_peer(d)).wait_send())
        loop(1, nz, lambda d: forward(a, d).wait_send())
        loop(1, n_dp, lambda d: col_copy(a, d).wait_send())


def expert_rows(e, chunk, coords, back, we, pin, gate, up, down, pout, acc):
    rows, rank = back.shape
    ff = gate.shape[2]
    scaled = (we * back).astype(bf16)
    codes = dot(coords, pin[e]).astype(bf16)
    d_narrow32 = dot_nt(scaled, pout[e])
    d_narrow = d_narrow32.astype(bf16)
    codes_t, d_narrow_t = codes.T, d_narrow.T
    narrow32 = jnp.zeros((rows, LANES), f32)
    d_codes32 = jnp.zeros((rows, LANES), f32)
    for at in range(0, ff, chunk):
        now = slice(at, at + chunk)
        gate_pre = dot(codes, gate[e, :, now])
        up_pre = dot(codes, up[e, :, now])
        d_hidden = dot_nt(d_narrow, down[e, now, :])
        sig = 0.5 * jnp.tanh(0.5 * gate_pre) + 0.5
        active = gate_pre * sig
        slope = sig + active * (1.0 - sig)
        hidden = (active * up_pre).astype(bf16)
        d_gate = (d_hidden * up_pre * slope).astype(bf16)
        d_up = (d_hidden * active).astype(bf16)
        narrow32 += dot(hidden, down[e, now, :])
        d_codes32 += dot_nt(d_gate, gate[e, :, now]) + dot_nt(d_up, up[e, :, now])
        acc[e, :, at : at + chunk] += dot(codes_t, d_gate)
        acc[e, :, ff + at : ff + at + chunk] += dot(codes_t, d_up)
        acc[e, :, 2 * ff + at : 2 * ff + at + chunk] += dot(d_narrow_t, hidden)
    narrow = narrow32.astype(bf16)
    d_codes = d_codes32.astype(bf16)
    outcome = dot(narrow, pout[e]).astype(bf16)
    acc[e, :, 3 * ff : 3 * ff + rank] += dot(d_codes.T, coords)
    acc[e, :, 3 * ff + rank :] += dot(narrow.T, scaled)
    sums = lax.dot_general(
        jnp.ones((8, LANES), f32),
        narrow.astype(f32) * d_narrow32,
        (((1,), (1,)), ((), ())),
        precision=lax.Precision.HIGHEST,
        preferred_element_type=f32,
    )
    return we * outcome.astype(f32), dot_nt(d_codes, pin[e]), sums


def pack(n_dp, ff, rank, e, acc, packed):
    wide, deep = ff // n_dp, rank // n_dp
    for q in range(n_dp):
        starts = [3 * ff + q * deep + i for i in range(0, deep, LANES)]
        for base in (0, ff, 2 * ff):
            starts += [base + q * wide + i for i in range(0, wide, LANES)]
        starts += [3 * ff + rank + q * deep + i for i in range(0, deep, LANES)]
        for i, at in enumerate(starts):
            packed[q, e, i] = acc[e, :, at : at + LANES].astype(bf16)


def expert_kernel(n_dp, chunk, x, w, pin, gate, up, down, pout, part, route, packed, acc):
    step = pl.program_id(0)
    nb, rank = x.shape[0], x.shape[3]
    rows = nb * TOK_DEV
    ff = gate.shape[2]

    @pl.when(step == 0)
    def _():
        acc[...] = jnp.zeros_like(acc)

    coords = x[:, 0].reshape(rows, rank)
    back = x[:, 1].reshape(rows, rank).astype(f32)
    dz = jnp.zeros((rows, rank), f32)
    mixed = jnp.zeros((rows, rank), f32)
    dots = jnp.zeros((8, rows), f32)
    line = lax.broadcasted_iota(jnp.int32, (8, rows), 0)
    for e in range(EXP_DEV):
        m, g, sums = expert_rows(
            e, chunk, coords, back, w[:, e : e + 1], pin, gate, up, down, pout, acc
        )
        mixed += m
        dz += g
        dots = jnp.where(line == e, sums, dots)
    part[:, 0] = dz.astype(bf16).reshape(nb, TOK_DEV, rank)
    part[:, 1] = mixed.astype(bf16).reshape(nb, TOK_DEV, rank)
    for b in range(nb):
        route[b] = dots[:, b * TOK_DEV : (b + 1) * TOK_DEV]

    @pl.when(step == pl.num_programs(0) - 1)
    def _():
        for e in range(EXP_DEV):
            pack(n_dp, ff, rank, e, acc, packed)


def expert_sum(n, me, part, held, landed, total, s1, r1, s2, r2):
    nz = n // 2
    core, z = lax.rem(me, 2), me // 2
    sib = me + 1 - 2 * core

    def to_sib(k):
        return remote(part.at[k * 2 + 1 - core], held.at[k], s1.at[k], r1.at[k], expert=sib)

    def to_line(d):
        k = lax.rem(z + d, nz)
        return remote(held.at[k], landed.at[z], s2.at[d], r2.at[z], expert=k * 2 + core)

    loop(1, nz, lambda d: to_sib(lax.rem(z + d, nz)).start())
    to_sib(z).start()

    def add(d):
        k = lax.rem(z + d, nz)
        to_sib(k).wait_recv()
        held[k] = (part[k * 2 + core].astype(f32) + held[k].astype(f32)).astype(bf16)
        to_line(d).start()

    loop(1, nz, add)
    to_sib(z).wait_recv()
    total[...] = part[me].astype(f32) + held[z].astype(f32)

    def collect(d):
        k = lax.rem(z + nz - d, nz)
        remote(held.at[k], landed.at[k], s2.at[d], r2.at[k], expert=k * 2 + core).wait_recv()
        total[...] += landed[k].astype(f32)

    loop(1, nz, collect)
    loop(0, nz, lambda k: to_sib(k).wait_send())
    loop(1, nz, lambda d: to_line(d).wait_send())


def combine_kernel(
    n,
    n_dp,
    part,
    route,
    packed,
    cols,
    basis,
    grad_input,
    grad_basis,
    grads,
    route_out,
    held,
    landed,
    total,
    dzm,
    block,
    held_b,
    landed_b,
    grads_in,
    s_g,
    r_g,
    s_r,
    r_r,
    s1,
    r1,
    s2,
    r2,
    s_d,
    r_d,
    t1,
    q1,
    t2,
    q2,
):
    me, p = lax.axis_index("expert"), lax.axis_index("dp")
    rank = basis.shape[1]
    greet(n, n_dp, me, p)

    def route_copy(d):
        j = lax.rem(me + d, n)
        return remote(route.at[j], route_out.at[me], s_r.at[d], r_r.at[me], expert=j)

    def grad_copy(d):
        q = lax.rem(p + d, n_dp)
        return remote(packed.at[q], grads_in.at[p], s_g.at[d], r_g.at[p], dp=q)

    loop(1, n, lambda d: route_copy(d).start())
    loop(1, n_dp, lambda d: grad_copy(d).start())
    route_out[me] = route[me]
    expert_sum(n, me, part, held, landed, total, s1, r1, s2, r2)
    dzm[p] = total[...].astype(bf16)

    def dzm_copy(d):
        q = lax.rem(p + d, n_dp)
        return remote(dzm.at[p], dzm.at[p], s_d.at[d], r_d.at[p], dp=q)

    loop(1, n_dp, lambda d: dzm_copy(d).start())
    grad_input[...] = dot_nt(dzm[p, 0], basis[...]).astype(bf16)

    def dzm_wait(d):
        src = lax.rem(p + n_dp - d, n_dp)
        remote(dzm.at[src], dzm.at[src], s_d.at[d], r_d.at[src], dp=src).wait_recv()

    loop(1, n_dp, dzm_wait)
    tokens = n_dp * 2 * TOK_DEV
    width = cols.shape[3]
    sums = dot_tn(cols[...].reshape(tokens, width), dzm[...].reshape(tokens, rank))
    block[...] = sums.astype(bf16).reshape(block.shape)
    expert_sum(n, me, block, held_b, landed_b, grad_basis, t1, q1, t2, q2)

    def grad_wait(d):
        src = lax.rem(p + n_dp - d, n_dp)
        remote(grads_in.at[src], grads_in.at[src], s_g.at[d], r_g.at[src], dp=src).wait_recv()
        grads[...] += grads_in[src].astype(f32)

    grads[...] = packed[p].astype(f32)
    loop(1, n_dp, grad_wait)

    def route_wait(d):
        src = lax.rem(me + n - d, n)
        remote(route.at[src], route_out.at[src], s_r.at[d], r_r.at[src], expert=src).wait_recv()

    loop(1, n, route_wait)
    loop(1, n, lambda d: route_copy(d).wait_send())
    loop(1, n_dp, lambda d: grad_copy(d).wait_send())
    loop(1, n_dp, lambda d: dzm_copy(d).wait_send())


def crossed(z, d, nz):
    k, bit = 0, 1
    while bit < nz:
        zb, db = lax.rem(z // bit, 2), lax.rem(d // bit, 2)
        k = k + bit * (zb + db - 2 * zb * db)
        bit *= 2
    return k


def layer_kernel(
    n, n_dp, chunk,
    act_h, cot_h, basis_h, wt, pin_h, pout_h, gate_h, up_h, down_h,
    grad_input, grad_basis, grads, route_out,
    act, cot, basis, pin, pout, gate, up, down,
    x, w_in, cols, cols_t, acc, part, route, packed, grads_in,
    held, landed, total, dzm, block, held_b, landed_b,
    s_l, s_c, r_c, s_x, r_x, s_f, s_w, r_w, s_g, r_g, s_r, r_r,
    s1, r1, s2, r2, s_d, r_d, t1, q1, t2, q2,
):
    me, p = lax.axis_index("expert"), lax.axis_index("dp")
    nz = n // 2
    core, z = lax.rem(me, 2), me // 2
    sib = me + 1 - 2 * core
    rank = basis.shape[1]
    ff = gate.shape[2]
    width = act.shape[1] // n_dp
    rows = 2 * TOK_DEV

    loads = [
        pltpu.make_async_copy(src, dst, s_l.at[i])
        for i, (src, dst) in enumerate(
            zip(
                (act_h, basis_h, cot_h, pin_h, pout_h, gate_h, up_h, down_h),
                (act, basis, cot, pin, pout, gate, up, down),
            )
        )
    ]
    for load in loads:
        load.start()
    greet(n, n_dp, me, p)

    def w_copy(d):
        j = lax.rem(me + d, n)
        return remote(wt.at[j], w_in.at[me], s_w.at[d], r_w.at[me], expert=j)

    loop(1, n, lambda d: w_copy(d).start())

    def peer(d):
        return crossed(z, d, nz)

    def x_copy(a, d, to):
        return remote(x.at[me, a], x.at[me, a], s_x.at[a, d], r_x.at[a, me], expert=to)

    near = 3 if nz == 4 else nz

    def relay(a):
        src = peer(2) * 2 + core
        return remote(
            x.at[src, a], x.at[src, a], s_x.at[a, 3], r_x.at[a, src], expert=peer(1) * 2 + core
        )

    loads[0].wait()
    loads[1].wait()
    for a, ref in enumerate((act, cot)):
        if a == 1:
            loads[2].wait()
        x[me, a] = dot(ref[...], basis[...]).astype(bf16)
        x_copy(a, 0, sib).start()
        loop(1, near, lambda d: x_copy(a, d, peer(d) * 2 + core).start())

    def col_copy(a, d):
        q = lax.rem(p + d, n_dp)
        return remote(
            (act, cot)[a].at[:, pl.ds(pl.multiple_of(q * width, LANES), width)],
            cols.at[p, a],
            s_c.at[a, d],
            r_c.at[a, p],
            dp=q,
        )

    for a in range(2):
        loop(1, n_dp, lambda d: col_copy(a, d).start())
    for a, ref in enumerate((act, cot)):
        cols[p, a] = ref[:, pl.ds(pl.multiple_of(p * width, LANES), width)]
    w_in[me] = wt[me]
    acc[...] = jnp.zeros_like(acc)

    def w_wait(d):
        src = lax.rem(me + n - d, n)
        remote(wt.at[src], w_in.at[src], s_w.at[d], r_w.at[src], expert=src).wait_recv()

    loop(1, n, w_wait)
    for load in loads[3:]:
        load.wait()

    def forward(a, d):
        src = peer(d) * 2 + core
        return remote(x.at[src, a], x.at[src, a], s_f.at[a, d], r_x.at[a, src], expert=sib)

    def from_sib(a, d):
        src = peer(d) * 2 + 1 - core
        return remote(x.at[src, a], x.at[src, a], s_f.at[a, d], r_x.at[a, src], expert=sib)

    def to_sib(k):
        return remote(part.at[k * 2 + 1 - core], held.at[k], s1.at[k], r1.at[k], expert=sib)

    def to_line(d):
        k = peer(d)
        return remote(held.at[k], landed.at[z], s2.at[d], r2.at[z], expert=k * 2 + core)

    def combine(d):
        k = peer(d)
        to_sib(k).wait_recv()
        held[k] = (part[k * 2 + core].astype(f32) + held[k].astype(f32)).astype(bf16)
        to_line(d).start()

    def grad_copy(e, d):
        q = lax.rem(p + d, n_dp)
        return remote(packed.at[q, e], grads_in.at[p, e], s_g.at[e, d], r_g.at[e, p], dp=q)

    early = max(1, n_dp - 1)

    def send_grads(e):
        pack(n_dp, ff, rank, e, acc, packed)
        loop(1, early, lambda d: grad_copy(e, d).start())

    line = lax.broadcasted_iota(jnp.int32, (8, rows), 0)
    square = (TOK_DEV, TOK_DEV)
    eye = lax.broadcasted_iota(jnp.int32, square, 0) == lax.broadcasted_iota(jnp.int32, square, 1)

    def pair(d):
        k = peer(d)

        @pl.when(d > 0)
        def _():
            for a in range(2):
                forward(a, d).wait_recv()
                forward(a, d).start()

        if near < nz:

            @pl.when(d == 2)
            def _():
                for a in range(2):
                    relay(a).start()

        for a in range(2):
            from_sib(a, d).wait_recv()
        both = pl.ds(k * 2, 2)
        coords = x[both, 0].reshape(rows, rank)
        back = x[both, 1].reshape(rows, rank).astype(f32)

        def column(e):
            return jnp.concatenate(
                [
                    jnp.sum(jnp.where(eye, w_in[k * 2 + b, e : e + 1, :], 0.0), axis=1, keepdims=True)
                    for b in range(2)
                ],
                axis=0,
            )

        @pl.when(d > 1)
        def _():
            combine(d - 1)

        mixed = jnp.zeros((rows, rank), f32)
        dz = jnp.zeros((rows, rank), f32)
        dots = jnp.zeros((8, rows), f32)
        for e in range(EXP_DEV):
            m, g, sums = expert_rows(
                e, chunk, coords, back, column(e), pin, gate, up, down, pout, acc
            )
            mixed += m
            dz += g
            dots = jnp.where(line == e, sums, dots)
        part[both, 0] = dz.astype(bf16).reshape(2, TOK_DEV, rank)
        part[both, 1] = mixed.astype(bf16).reshape(2, TOK_DEV, rank)
        for b in range(2):
            route[k * 2 + b] = dots[:, b * TOK_DEV : (b + 1) * TOK_DEV]
        to_sib(k).start()

    loop(0, nz, pair)
    send_grads(0)
    if nz > 1:
        combine(nz - 1)

    def route_copy(d):
        j = lax.rem(me + d, n)
        return remote(route.at[j], route_out.at[me], s_r.at[d], r_r.at[me], expert=j)

    loop(1, n, lambda d: route_copy(d).start())
    route_out[me] = route[me]
    for e in range(1, EXP_DEV):
        pack(n_dp, ff, rank, e, acc, packed)
    to_sib(z).wait_recv()
    total[...] = part[me].astype(f32) + held[z].astype(f32)

    def collect(d):
        k = peer(d)
        remote(held.at[k], landed.at[k], s2.at[d], r2.at[k], expert=k * 2 + core).wait_recv()
        total[...] += landed[k].astype(f32)

    loop(1, nz, collect)
    dzm[p] = total[...].astype(bf16)

    def dzm_copy(d):
        q = lax.rem(p + d, n_dp)
        return remote(dzm.at[p], dzm.at[p], s_d.at[d], r_d.at[p], dp=q)

    loop(1, n_dp, lambda d: dzm_copy(d).start())
    loop(early, n_dp, lambda d: grad_copy(0, d).start())
    for e in range(1, EXP_DEV):
        loop(1, n_dp, lambda d: grad_copy(e, d).start())

    def col_wait(a, d):
        src = lax.rem(p + n_dp - d, n_dp)
        remote(cols.at[src, a], cols.at[src, a], s_c.at[a, d], r_c.at[a, src], dp=src).wait_recv()

    for a in range(2):
        loop(1, n_dp, lambda d: col_wait(a, d))
    for q in range(n_dp):
        for a in range(2):
            at = (q * 2 + a) * TOK_DEV
            cols_t[:, at : at + TOK_DEV] = cols[q, a].T
    grad_input[...] = dot_nt(dzm[p, 0], basis[...]).astype(bf16)

    def dzm_wait(d):
        src = lax.rem(p + n_dp - d, n_dp)
        remote(dzm.at[src], dzm.at[src], s_d.at[d], r_d.at[src], dp=src).wait_recv()

    loop(1, n_dp, dzm_wait)
    sums = dot(cols_t[...], dzm[...].reshape(n_dp * rows, rank))
    block[...] = sums.astype(bf16).reshape(block.shape)
    expert_sum(n, me, block, held_b, landed_b, grad_basis, t1, q1, t2, q2)

    def grad_wait(e, d):
        src = lax.rem(p + n_dp - d, n_dp)
        remote(
            grads_in.at[src, e], grads_in.at[src, e], s_g.at[e, d], r_g.at[e, src], dp=src
        ).wait_recv()
        grads[e] += grads_in[src, e].astype(f32)

    for e in range(EXP_DEV):
        grads[e] = packed[p, e].astype(f32)
        loop(1, n_dp, lambda d: grad_wait(e, d))

    def route_wait(d):
        src = lax.rem(me + n - d, n)
        remote(route.at[src], route_out.at[src], s_r.at[d], r_r.at[src], expert=src).wait_recv()

    loop(1, n, route_wait)
    loop(1, n, lambda d: route_copy(d).wait_send())
    loop(1, n, lambda d: w_copy(d).wait_send())
    for a in range(2):
        x_copy(a, 0, sib).wait_send()
        loop(1, near, lambda d: x_copy(a, d, peer(d) * 2 + core).wait_send())
        if near < nz:
            relay(a).wait_send()
        loop(1, nz, lambda d: forward(a, d).wait_send())
        loop(1, n_dp, lambda d: col_copy(a, d).wait_send())
    loop(0, nz, lambda k: to_sib(k).wait_send())
    loop(1, nz, lambda d: to_line(d).wait_send())
    loop(1, n_dp, lambda d: dzm_copy(d).wait_send())
    for e in range(EXP_DEV):
        loop(1, n_dp, lambda d: grad_copy(e, d).wait_send())


def finish_kernel(
    gi, gb, grads, grad_input, grad_basis, g_in, g_gate, g_up, g_down, g_out,
):
    grad_input[...] = gi[...]
    grad_basis[...] = gb[...]
    deep, wide = g_in.shape[1] // LANES, g_gate.shape[2] // LANES
    for e in range(EXP_DEV):
        for i in range(deep):
            at = slice(i * LANES, (i + 1) * LANES)
            g_in[e, at, :] = grads[e, i].T
            g_out[e, :, at] = grads[e, deep + 3 * wide + i]
        for i in range(wide):
            at = slice(i * LANES, (i + 1) * LANES)
            g_gate[e, :, at] = grads[e, deep + i]
            g_up[e, :, at] = grads[e, deep + wide + i]
            g_down[e, at, :] = grads[e, deep + 2 * wide + i].T


def whole_layer(n, n_dp, shapes, blocks, arrays, wt):
    model, rank, ff = shapes
    nz = n // 2
    width = model // n_dp
    rows_b = width // n
    vmem = pl.BlockSpec(memory_space=pltpu.VMEM)
    hbm = pl.BlockSpec(memory_space=pl.ANY)
    dma = pltpu.SemaphoreType.DMA
    act, cot, basis, *weights = arrays
    token = (TOK_DEV, rank)
    return pl.pallas_call(
        functools.partial(layer_kernel, n, n_dp, ff // 3),
        out_shape=(
            jax.ShapeDtypeStruct((TOK_DEV, model), bf16),
            jax.ShapeDtypeStruct((rows_b, rank), f32),
            jax.ShapeDtypeStruct(blocks, f32),
            jax.ShapeDtypeStruct((n, 8, TOK_DEV), f32),
        ),
        in_specs=[hbm] * 3 + [vmem] + [hbm] * 5,
        out_specs=(vmem,) * 4,
        scratch_shapes=[pltpu.VMEM(a.shape, bf16) for a in arrays]
        + [
            pltpu.VMEM((n, 2, *token), bf16),
            pltpu.VMEM((n, 8, TOK_DEV), f32),
            pltpu.VMEM((n_dp, 2, TOK_DEV, width), bf16),
            pltpu.VMEM((width, n_dp * 2 * TOK_DEV), bf16),
            pltpu.VMEM((EXP_DEV, LANES, 3 * ff + 2 * rank), f32),
            pltpu.VMEM((n, 2, *token), bf16),
            pltpu.VMEM((n, 8, TOK_DEV), f32),
            pltpu.VMEM((n_dp, *blocks), bf16),
            pltpu.VMEM((n_dp, *blocks), bf16),
            pltpu.VMEM((nz, 2, *token), bf16),
            pltpu.VMEM((nz, 2, *token), bf16),
            pltpu.VMEM((2, *token), f32),
            pltpu.VMEM((n_dp, 2, *token), bf16),
            pltpu.VMEM((n, rows_b, rank), bf16),
            pltpu.VMEM((nz, rows_b, rank), bf16),
            pltpu.VMEM((nz, rows_b, rank), bf16),
        ]
        + [
            dma(s)
            for s in (
                (8,), (2, n_dp), (2, n_dp), (2, nz), (2, n), (2, nz), (n,), (n,),
                (EXP_DEV, n_dp), (EXP_DEV, n_dp), (n,), (n,),
                (nz,), (nz,), (nz,), (nz,), (n_dp,), (n_dp,), (nz,), (nz,), (nz,), (nz,),
            )
        ],
        compiler_params=pltpu.CompilerParams(
            collective_id=2, has_side_effects=True, vmem_limit_bytes=VMEM_LIMIT
        ),
        name="whole_layer",
    )(act, cot, basis, wt, *weights)


def staged_layer(n, n_dp, shapes, blocks, arrays, wt):
    model, rank, ff = shapes
    nz = n // 2
    width = model // n_dp
    vmem = pl.BlockSpec(memory_space=pltpu.VMEM)
    dma = pltpu.SemaphoreType.DMA
    activations, cotangent, basis, proj_in, proj_out, gate_factor, up_factor, down_factor = arrays
    x, w_all, cols = pl.pallas_call(
        functools.partial(gather_kernel, n, n_dp),
        out_shape=(
            jax.ShapeDtypeStruct((n, 2, TOK_DEV, rank), bf16),
            jax.ShapeDtypeStruct((n, 8, TOK_DEV), f32),
            jax.ShapeDtypeStruct((n_dp, 2, TOK_DEV, width), bf16),
        ),
        in_specs=[vmem] * 4,
        out_specs=(vmem,) * 3,
        scratch_shapes=[
            dma((2, n_dp)),
            dma((2, n_dp)),
            dma((2, nz)),
            dma((2, n)),
            dma((2, nz)),
            dma((n,)),
            dma((n,)),
        ],
        compiler_params=pltpu.CompilerParams(
            collective_id=0, has_side_effects=True, vmem_limit_bytes=VMEM_LIMIT
        ),
        name="gather_tokens",
    )(activations, cotangent, basis, wt)

    w_rows = w_all.transpose(0, 2, 1).reshape(n * TOK_DEV, 8)
    nb = 2
    whole = lambda a: pl.BlockSpec(a.shape, lambda i: (0,) * a.ndim)
    part, route, packed = pl.pallas_call(
        functools.partial(expert_kernel, n_dp, ff // 3),
        grid=(n // nb,),
        out_shape=(
            jax.ShapeDtypeStruct((n, 2, TOK_DEV, rank), bf16),
            jax.ShapeDtypeStruct((n, 8, TOK_DEV), f32),
            jax.ShapeDtypeStruct((n_dp, *blocks), bf16),
        ),
        in_specs=[
            pl.BlockSpec((nb, 2, TOK_DEV, rank), lambda i: (i, 0, 0, 0)),
            pl.BlockSpec((nb * TOK_DEV, 8), lambda i: (i, 0)),
            whole(proj_in),
            whole(gate_factor),
            whole(up_factor),
            whole(down_factor),
            whole(proj_out),
        ],
        out_specs=(
            pl.BlockSpec((nb, 2, TOK_DEV, rank), lambda i: (i, 0, 0, 0)),
            pl.BlockSpec((nb, 8, TOK_DEV), lambda i: (i, 0, 0)),
            pl.BlockSpec((n_dp, *blocks), lambda i: (0, 0, 0, 0, 0)),
        ),
        scratch_shapes=[pltpu.VMEM((EXP_DEV, LANES, 3 * ff + 2 * rank), f32)],
        compiler_params=pltpu.CompilerParams(vmem_limit_bytes=VMEM_LIMIT),
        name="experts",
    )(x, w_rows, proj_in, gate_factor, up_factor, down_factor, proj_out)

    rows_b = width // n
    return pl.pallas_call(
        functools.partial(combine_kernel, n, n_dp),
        out_shape=(
            jax.ShapeDtypeStruct((TOK_DEV, model), bf16),
            jax.ShapeDtypeStruct((rows_b, rank), f32),
            jax.ShapeDtypeStruct(blocks, f32),
            jax.ShapeDtypeStruct((n, 8, TOK_DEV), f32),
        ),
        in_specs=[vmem] * 5,
        out_specs=(vmem,) * 4,
        scratch_shapes=[
            pltpu.VMEM((nz, 2, TOK_DEV, rank), bf16),
            pltpu.VMEM((nz, 2, TOK_DEV, rank), bf16),
            pltpu.VMEM((2, TOK_DEV, rank), f32),
            pltpu.VMEM((n_dp, 2, TOK_DEV, rank), bf16),
            pltpu.VMEM((n, rows_b, rank), bf16),
            pltpu.VMEM((nz, rows_b, rank), bf16),
            pltpu.VMEM((nz, rows_b, rank), bf16),
            pltpu.VMEM((n_dp, *blocks), bf16),
            dma((n_dp,)),
            dma((n_dp,)),
            dma((n,)),
            dma((n,)),
            dma((nz,)),
            dma((nz,)),
            dma((nz,)),
            dma((nz,)),
            dma((n_dp,)),
            dma((n_dp,)),
            dma((nz,)),
            dma((nz,)),
            dma((nz,)),
            dma((nz,)),
        ],
        compiler_params=pltpu.CompilerParams(
            collective_id=1, has_side_effects=True, vmem_limit_bytes=VMEM_LIMIT
        ),
        name="combine",
    )(part, route, packed, cols, basis)


def per_device(
    n,
    n_dp,
    activations,
    cotangent,
    basis,
    route_ids,
    route_weights,
    proj_in,
    gate_factor,
    up_factor,
    down_factor,
    proj_out,
):
    model, rank = basis.shape
    ff = gate_factor.shape[2]
    experts = EXP_DEV * n

    chosen = route_ids[:, None, :] == jnp.arange(experts, dtype=jnp.int32)[None, :, None]
    dense = jnp.sum(jnp.where(chosen, route_weights[:, None, :], 0.0), axis=2)
    wt = dense.T.reshape(n, EXP_DEV, TOK_DEV)
    wt = jnp.pad(wt, ((0, 0), (0, 8 - EXP_DEV), (0, 0)))

    blocks = EXP_DEV, (2 * rank + 3 * ff) // n_dp // LANES, LANES, LANES
    arrays = activations, cotangent, basis, proj_in, proj_out, gate_factor, up_factor, down_factor
    tokens = n * TOK_DEV * rank * 2
    fits = 6 * tokens + 34 * 1024 * 1024 < VMEM_LIMIT and (n & (n - 1)) == 0
    layer = whole_layer if fits else staged_layer
    grad_input, grad_basis, grads, dots = layer(n, n_dp, (model, rank, ff), blocks, arrays, wt)
    deep, wide = rank // n_dp, ff // n_dp
    vmem = pl.BlockSpec(memory_space=pltpu.VMEM)
    grad_input, grad_basis, *factors = pl.pallas_call(
        finish_kernel,
        out_shape=(
            jax.ShapeDtypeStruct(grad_input.shape, bf16),
            jax.ShapeDtypeStruct(grad_basis.shape, f32),
            jax.ShapeDtypeStruct((EXP_DEV, deep, LANES), f32),
            jax.ShapeDtypeStruct((EXP_DEV, LANES, wide), f32),
            jax.ShapeDtypeStruct((EXP_DEV, LANES, wide), f32),
            jax.ShapeDtypeStruct((EXP_DEV, wide, LANES), f32),
            jax.ShapeDtypeStruct((EXP_DEV, LANES, deep), f32),
        ),
        in_specs=[vmem] * 3,
        out_specs=(vmem,) * 7,
        compiler_params=pltpu.CompilerParams(vmem_limit_bytes=VMEM_LIMIT),
        name="finish",
    )(grad_input, grad_basis, grads)
    dots = dots[:, :EXP_DEV].reshape(experts, TOK_DEV).T
    grad_route = jnp.sum(jnp.where(chosen, dots[:, :, None], 0.0), axis=1) / route_weights
    return (grad_input, grad_route, grad_basis, *factors)


def solution(mesh):
    split = P(("dp", "expert"), None)
    held = P("expert", None, None)
    in_specs = (split, split, P(), split, split, held, held, held, held, held)
    out_specs = (
        split,
        split,
        split,
        P("expert", "dp", None),
        P("expert", None, "dp"),
        P("expert", None, "dp"),
        P("expert", "dp", None),
        P("expert", None, "dp"),
    )
    return jax.shard_map(
        functools.partial(per_device, mesh.shape["expert"], mesh.shape["dp"]),
        mesh=mesh,
        in_specs=in_specs,
        out_specs=out_specs,
        check_vma=False,
    )
```
